256 devices in a mesh: clip: 16 (over z, x_lo), tm: 16 (over y, x_hi, core).
Axes of the slice: x: 4 (x_hi: 2, x_lo: 2; x = x_hi * 2 + x_lo), y: 4, z: 8, core: 2. Of those that a mesh axis runs over, the one named last changes fastest.
Arguments:
- clip_embed: bfloat16 [6144, 512], P('clip'), may hold values from -0.1875 to 0.1875
- seg_feats: bfloat16 [16, 6144, 512], P('tm', 'clip'), may hold values from -1 to 1
- pair_index: int32 [16, 6144], P('tm', 'clip'), may hold values from 0 to 6143, as said below
Outputs:
- row_loss: float32 [16, 6144], P('tm', 'clip')
- grad_seg: float32 [16, 6144, 512], P('tm', 'clip')
- grad_clip: float32 [6144, 512], P('clip')
The draws below stay inside these ranges and needn't reach their ends.
Inputs may be any that keep to these rules, and one draw needn't show every extreme that they name: pair_index pairs the rows of each segment: pair_index[t, i] != i and pair_index[t, pair_index[t, i]] = i.
All inputs are finite; a program needn't handle non-finite values.
Results may differ from the reference program's by a relative error of at most 0.0029.
Values may be sent and summed in bfloat16 or wider, within the bound.
A program may use at most 128 MiB of HBM per device.

```python
import jax
import jax.numpy as jnp
from jax import lax

E = 512
CLIPS = 6144
SEGS = 16


def draw_pair_index(key, part):
    key = jax.random.fold_in(key, 11)
    seg_keys = jax.random.split(key, SEGS)
    orders = jax.vmap(lambda single: jax.random.permutation(single, CLIPS))(seg_keys).astype(jnp.int32)
    leading = orders[:, 0::2]
    trailing = orders[:, 1::2]
    segment_ids = jnp.arange(SEGS, dtype=jnp.int32)[:, None]
    result = jnp.zeros((SEGS, CLIPS), jnp.int32)
    result = result.at[segment_ids, leading].set(trailing)
    return result.at[segment_ids, trailing].set(leading)


def draw_seg_feats(key, part):
    key = jax.random.fold_in(key, 23)
    order_key, family_key, strength_key, noise_key, basis_key, coef_key, mix_key = jax.random.split(key, 7)
    seg_keys = jax.random.split(order_key, SEGS)
    orders = jax.vmap(lambda single: jax.random.permutation(single, CLIPS))(seg_keys).astype(jnp.int32)
    places = jnp.arange(CLIPS, dtype=jnp.int32)
    family_of_place = places // 12
    segment_ids = jnp.arange(SEGS, dtype=jnp.int32)[:, None]
    family = jnp.zeros((SEGS, CLIPS), jnp.int32).at[segment_ids, orders].set(jnp.broadcast_to(family_of_place, (SEGS, CLIPS)))
    vectors = jax.random.normal(family_key, (SEGS, CLIPS, E), jnp.float32)
    strength = jax.random.uniform(strength_key, (SEGS, CLIPS), jnp.float32, 1.0, 6.0)
    noise = 0.70710678 * jax.random.normal(noise_key, (SEGS, CLIPS, E), jnp.float32)
    basis = jax.random.normal(basis_key, (SEGS, 8, E), jnp.float32)
    coefs = jax.random.normal(coef_key, (SEGS, CLIPS, 8), jnp.float32)
    mixing = jnp.exp(jax.random.uniform(mix_key, (SEGS, CLIPS), jnp.float32, -1.6094379, -0.6931472))
    picked_vectors = jax.vmap(lambda table, index: jnp.take(table, index, axis=0))(vectors, family)
    scaled_coefs = coefs * mixing[:, :, None]
    shared = jnp.zeros((SEGS, CLIPS, E), jnp.float32)
    for component in range(8):
        shared = shared + scaled_coefs[:, :, component, None] * basis[:, None, component, :]
    inverse_root = 1.0 / jnp.sqrt(jnp.float32(E))
    row_scale = jnp.sqrt(strength) * inverse_root
    values = picked_vectors * row_scale[:, :, None] + (shared + noise) * inverse_root
    return jnp.clip(values, -1.0, 1.0).astype(jnp.bfloat16)


def block_levels(rng, extent, cuts, smallest, top_value):
    gain, own = 1.0, jax.random.fold_in(rng, 6)
    for axis_at, shards_of in cuts:
        heights = jnp.exp(jax.random.uniform(jax.random.fold_in(own, axis_at), (shards_of,), jnp.float32, smallest / len(cuts), top_value / len(cuts)))
        gain = gain * jnp.repeat(heights, extent[axis_at] // shards_of).reshape([-1 if axis == axis_at else 1 for axis in range(len(extent))])
    return gain


def centred(stream_key, extent, scale, reach, cuts=(), kind=jnp.bfloat16):
    drawn = jax.random.normal(stream_key, extent, jnp.float32) * scale
    if len(cuts) > 0:
        drawn = block_levels(stream_key, extent, cuts, -0.22, 0.18) * drawn
    return jnp.clip(drawn, min=-reach, max=reach).astype(kind)


def setup_inputs(seed: int = 0) -> dict:
    streams_of = jax.random.split(jax.random.key(seed), 4)
    clip_embed = centred(streams_of[0], (CLIPS, E), (2 * E) ** -0.5, 0.1875, ((0, 16),))
    seg_feats = draw_seg_feats(jax.random.fold_in(streams_of[3], 71), 0)
    pair_index = draw_pair_index(jax.random.fold_in(streams_of[3], 71), 0)
    return {"clip_embed": clip_embed, "seg_feats": seg_feats, "pair_index": pair_index}


logit_scale = 14.0
norm_eps = 1e-06

def one_segment(items):
    clip_embed, features, partners = items
    summed = clip_embed.astype(jnp.float32) + features.astype(jnp.float32)
    factor = lax.rsqrt(lax.optimization_barrier(jnp.sum(summed * summed, 1, keepdims=True)) + E * norm_eps)
    unit = (summed * factor).astype(jnp.bfloat16)
    score = jnp.dot(unit, unit.T, preferred_element_type=jnp.float32)
    positions = jnp.arange(CLIPS, dtype=jnp.int32)
    off_diagonal = positions[:, None] != positions[None, :]
    expo = jnp.where(off_diagonal, jnp.exp(logit_scale * (score - 1.0)), 0.0)
    totals = lax.optimization_barrier(jnp.sum(expo, 1))
    positive = jnp.take_along_axis(score, partners[:, None], 1)[:, 0]
    row_loss = logit_scale * (1.0 - positive) + jnp.log(totals)
    inverse = 1.0 / totals
    weights = expo * (inverse[:, None] + inverse[None, :])
    pulled = jnp.dot(weights, unit.astype(jnp.float32), precision=lax.Precision.HIGHEST, preferred_element_type=jnp.float32)
    partner_rows = jnp.take(unit, partners, axis=0).astype(jnp.float32)
    grad_unit = logit_scale * (pulled - 2.0 * partner_rows)
    along = lax.optimization_barrier(jnp.sum(summed * grad_unit, 1, keepdims=True))
    grad_seg = factor * grad_unit - factor ** 3 * summed * along
    return (row_loss, grad_seg)

def reference(clip_embed, seg_feats, pair_index):

    def mapped(items):
        return one_segment((clip_embed, items[0], items[1]))
    row_loss, grad_seg = lax.map(mapped, (seg_feats, pair_index))
    grad_clip = lax.optimization_barrier(jnp.sum(grad_seg, 0))
    return (row_loss, grad_seg, grad_clip)
```

```python
import functools
import math

import jax
import jax.numpy as jnp
from jax import lax
from jax.experimental import pallas as pl
from jax.experimental.pallas import tpu as pltpu
from jax.sharding import PartitionSpec as P

MESH = pl.DeviceIdType.MESH
logit_scale = 14.0
norm_eps = 1e-06
exp2_scale = logit_scale * math.log2(math.e)

ZS = 8
ROWS = 384
HALF = ROWS // 2
PAIR = 2 * ROWS
E = 512
PEERS = 8
PIECE = ROWS // PEERS
STEPS = ZS


def remote(src, dst, send_sem, recv_sem, device):
    return pltpu.make_async_remote_copy(
        src_ref=src, dst_ref=dst, send_sem=send_sem, recv_sem=recv_sem,
        device_id=device, device_id_type=MESH,
    )


def dot(a, b):
    return jnp.dot(a, b, preferred_element_type=jnp.float32)


def kernel(
    clip_ref, feat_ref, pair_ref,
    loss_out, seg_out, clip_out,
    u_all, ut_all, expo_all, tot_all, unit_t, stage, raw_clip, raw_feat, partner, totals,
    pull_one, pull_pos, acc, summed_t, ret_stage, ret, sib_grad, loss_stage, loss_ret,
    rs_send, rs_buf, gathered,
    swap_s, swap_r, ring_s, ring_r, sib_s, sib_r, tot_s, tot_r, ret_s, ret_r, grad_s, grad_r,
    rs_s, rs_r, ag_s, ag_r, fin_s, fin_r,
):
    clip = lax.axis_index("clip")
    tm = lax.axis_index("tm")
    z, x = clip // 2, lax.rem(clip, 2)
    peer, core = tm // 2, lax.rem(tm, 2)
    stays = x == core
    moves = x != core

    def at(zz, xx, pp, cc):
        return (zz * 2 + xx, pp * 2 + cc)

    def ring(offset):
        return lax.rem(z + offset + ZS, ZS)

    sibling = at(z, x, peer, 1 - core)
    swapped = at(z, 1 - x, peer, 1 - core)

    barrier = pltpu.get_barrier_semaphore()

    def greet(device):
        pl.semaphore_signal(barrier, inc=1, device_id=device, device_id_type=MESH)

    for dz in range(ZS):
        for dc in range(2):
            if dz or dc:
                greet(at(ring(dz), x, peer, lax.rem(core + dc, 2)))

    @pl.when(moves)
    def _():
        greet(swapped)
        for d in range(1, PEERS):
            greet(at(z, x, lax.rem(peer + d, PEERS), core))

    summed = clip_ref[...].astype(jnp.float32) + feat_ref[0].astype(jnp.float32)
    factor = lax.rsqrt(jnp.sum(summed * summed, 1, keepdims=True) + E * norm_eps)
    unit = (summed * factor).astype(jnp.bfloat16)

    def half(zz, block, which):
        return u_all.at[zz, pl.ds(pl.multiple_of(block * ROWS + which * HALF, HALF), HALF)]

    def swap_copies():
        return [
            remote(stage.at[pl.ds(0, HALF)], half(z, x, 0), swap_s.at[0], swap_r.at[0], swapped),
            remote(stage.at[pl.ds(HALF, HALF)], half(z, x, 1), swap_s.at[1], swap_r.at[1], swapped),
            remote(pair_ref, partner, swap_s.at[2], swap_r.at[2], swapped),
            remote(feat_ref.at[0], raw_feat, swap_s.at[3], swap_r.at[3], swapped),
            remote(clip_ref, raw_clip, swap_s.at[4], swap_r.at[4], swapped),
        ]

    def swap_waits():
        copies = swap_copies()
        copies[0] = remote(stage.at[pl.ds(0, HALF)], half(z, core, 0), swap_s.at[0], swap_r.at[0], swapped)
        copies[1] = remote(stage.at[pl.ds(HALF, HALF)], half(z, core, 1), swap_s.at[1], swap_r.at[1], swapped)
        return copies

    def ring_copy(way, hop, order):
        if way == 0:
            source, target, which = ring(-hop), ring(1), order
        else:
            source, target, which = ring(hop), ring(-1), 1 - order
        ref = half(source, core, which)
        index = 2 * hop + order
        return remote(ref, ref, ring_s.at[way, index], ring_r.at[way, index], at(target, x, peer, core))

    def ring_arrival(way, hop, order):
        source, which = (ring(-hop), order) if way == 0 else (ring(hop), 1 - order)
        ref = half(source, core, which)
        index = 2 * (hop - 1) + order
        return remote(ref, ref, ring_s.at[way, index], ring_r.at[way, index], sibling), source, which

    def sib_copy(source, which):
        ref = half(source, core, which)
        return remote(ref, ref, sib_s.at[source, which], sib_r.at[source, which], sibling)

    def sib_arrival(source, which):
        ref = half(source, 1 - core, which)
        return remote(ref, ref, sib_s.at[source, which], sib_r.at[source, which], sibling)

    @pl.when(stays)
    def _():
        u_all[z, pl.ds(pl.multiple_of(core * ROWS, ROWS), ROWS), :] = unit
        raw_clip[...] = clip_ref[...]
        raw_feat[...] = feat_ref[0]
        partner[...] = pair_ref[...]
        pl.semaphore_wait(barrier, 2 * ZS - 1)

    @pl.when(moves)
    def _():
        stage[...] = unit
        pl.semaphore_wait(barrier, 2 * ZS - 1 + PEERS)
        for copy in swap_copies():
            copy.start()
        waits = swap_waits()
        for copy in waits[:3]:
            copy.wait_recv()

    for order in range(2):
        for way in range(2):
            ring_copy(way, 0, order).start()
    for which in range(2):
        sib_copy(z, which).start()

    unit_t[...] = u_all[z, pl.ds(pl.multiple_of(core * ROWS, ROWS), ROWS), :].T
    totals[...] = jnp.zeros_like(totals)
    pull_one[...] = jnp.zeros_like(pull_one)
    pull_pos[...] = jnp.zeros_like(pull_pos)

    def column_ids(zz):
        return lax.broadcasted_iota(jnp.int32, (PAIR, ROWS), 0) + zz * PAIR

    def block_of(step):
        hop = (step + 1) // 2
        return ring(jnp.where(lax.rem(step, 2) == 1, -hop, hop))

    def score_part(zz):
        score = dot(u_all[zz], unit_t[...])
        own = lax.broadcasted_iota(jnp.int32, (1, ROWS), 1) + (z * PAIR + core * ROWS)
        expo = jnp.where(column_ids(zz) != own, jnp.exp2(score * exp2_scale - exp2_scale), 0.0)
        totals[...] += jnp.sum(expo, 0, keepdims=True)
        expo_all[zz] = expo.astype(jnp.bfloat16)

    def pull_part(zz):
        ut_all[zz] = u_all[zz].T
        picked = jnp.where(column_ids(zz) == partner[...], 1.0, 0.0).astype(jnp.bfloat16)
        pull_one[...] += dot(ut_all[zz], expo_all[zz])
        pull_pos[...] += dot(ut_all[zz], picked)

    def pass_on(way, hop, order, last_hop):
        arrival, source, which = ring_arrival(way, hop, order)
        arrival.wait_recv()

        @pl.when(hop <= last_hop)
        def _():
            ring_copy(way, hop, order).start()

        sib_copy(source, which).start()

    def gather_step(step, carry):
        hop = (step + 1) // 2

        @pl.when(lax.rem(step, 2) == 1)
        def _():
            for way in range(2):
                pass_on(way, hop, 0, 3)

            @pl.when(hop <= 3)
            def _():
                for way in range(2):
                    pass_on(way, hop, 1, 2)

        zz = block_of(step)

        @pl.when(step > 0)
        def _():
            pull_part(block_of(step - 1))

        for which in range(2):
            sib_arrival(zz, which).wait_recv()
        score_part(zz)
        return carry

    lax.fori_loop(0, STEPS, gather_step, 0)

    tot_all[z, core] = totals[...]

    def total_copies():
        copies = []
        for dz in (4, 3, 5, 2, 6, 1, 7, 0):
            for dc in range(2):
                if dz or dc:
                    copies.append(remote(
                        tot_all.at[z, core], tot_all.at[z, core], tot_s.at[dz, dc], tot_r.at[z, core],
                        at(ring(dz), x, peer, lax.rem(core + dc, 2)),
                    ))
        return copies

    for copy in total_copies():
        copy.start()

    pull_part(block_of(STEPS - 1))

    inverse = 1.0 / totals[...]
    positive = jnp.sum(unit_t[...].astype(jnp.float32) * pull_pos[...], 0, keepdims=True)
    loss = logit_scale * (1.0 - positive) + jnp.log(totals[...])
    loss_copy = remote(loss_stage, loss_ret, ret_s.at[3], ret_r.at[3], swapped)

    @pl.when(stays)
    def _():
        loss_out[...] = loss

    @pl.when(moves)
    def _():
        loss_stage[...] = loss
        loss_copy.start()
        waits = swap_waits()
        for copy in waits[3:]:
            copy.wait_recv()

    acc[...] = inverse * pull_one[...] - 2.0 * pull_pos[...]
    summed_t[...] = (raw_clip[...].astype(jnp.float32) + raw_feat[...].astype(jnp.float32)).T

    def total_arrival(zz, block):
        ref = tot_all.at[zz, block]
        return remote(ref, ref, tot_s.at[0, 0], tot_r.at[zz, block], sibling)

    def second_step(step, carry):
        zz = block_of(step)

        @pl.when(step > 0)
        def _():
            total_arrival(zz, core).wait_recv()

        total_arrival(zz, 1 - core).wait_recv()
        scale = 1.0 / jnp.concatenate([tot_all[zz, 0], tot_all[zz, 1]], 1)
        scaled = (ut_all[zz].astype(jnp.float32) * scale).astype(jnp.bfloat16)
        acc[...] += dot(scaled, expo_all[zz])
        return carry

    lax.fori_loop(0, STEPS, second_step, 0)

    factor_t = lax.rsqrt(jnp.sum(summed_t[...] * summed_t[...], 0, keepdims=True) + E * norm_eps)
    width = ROWS // 3

    def ret_copy(part):
        rows = pl.ds(part * width, width)
        return remote(ret_stage.at[rows], ret.at[rows], ret_s.at[part], ret_r.at[part], swapped)

    def grad_copy(part):
        rows = pl.ds(part * width, width)
        return remote(seg_out.at[0, rows], sib_grad.at[rows], grad_s.at[part], grad_r.at[part], sibling)

    for part in range(3):
        lanes = slice(part * width, (part + 1) * width)
        grad_unit = logit_scale * acc[:, lanes]
        summed_part = summed_t[:, lanes]
        factor_part = factor_t[:, lanes]
        along = jnp.sum(summed_part * grad_unit, 0, keepdims=True)
        grad = (factor_part * grad_unit - factor_part**3 * along * summed_part).T

        @pl.when(stays)
        def _():
            seg_out[0, lanes, :] = grad
            grad_copy(part).start()

        @pl.when(moves)
        def _():
            ret_stage[lanes, :] = grad.astype(jnp.bfloat16)
            ret_copy(part).start()

    def rs_copy(piece):
        target = at(z, x, piece, core)
        rows = pl.ds(piece * PIECE, PIECE)
        return remote(rs_send.at[rows], rs_buf.at[peer], rs_s.at[piece], rs_r.at[peer], target)

    def rs_arrival(source):
        ref = rs_buf.at[source]
        return remote(ref, ref, rs_s.at[0], rs_r.at[source], sibling)

    def gathered_rows(piece):
        return gathered.at[pl.ds(pl.multiple_of(piece * PIECE, PIECE), PIECE)]

    def ag_copy(d):
        target = at(z, x, lax.rem(peer + d, PEERS), core)
        ref = gathered_rows(peer)
        return remote(ref, ref, ag_s.at[d], ag_r.at[peer], target)

    def ag_arrival(source):
        ref = gathered_rows(source)
        return remote(ref, ref, ag_s.at[0], ag_r.at[source], sibling)

    def fin_copy(piece):
        ref = gathered_rows(piece)
        return remote(ref, ref, fin_s.at[piece], fin_r.at[piece], sibling)

    @pl.when(moves)
    def _():
        loss_copy.wait_recv()
        loss_out[...] = loss_ret[...]
        first_piece = 0
        for part in range(3):
            rows = slice(part * width, (part + 1) * width)
            ret_copy(part).wait_recv()
            grad_copy(part).wait_recv()
            home = ret[rows, :].astype(jnp.float32)
            seg_out[0, rows, :] = home
            rs_send[rows, :] = (home + sib_grad[rows, :]).astype(jnp.bfloat16)
            last_piece = (part + 1) * width // PIECE
            for piece in range(first_piece, last_piece):
                @pl.when(piece != peer)
                def _():
                    rs_copy(piece).start()

                @pl.when(piece == peer)
                def _():
                    rs_buf[peer] = rs_send[piece * PIECE:(piece + 1) * PIECE, :]
            first_piece = last_piece
        for d in range(1, PEERS):
            rs_arrival(lax.rem(peer + d, PEERS)).wait_recv()
        reduced = rs_buf[0].astype(jnp.float32)
        for source in range(1, PEERS):
            reduced += rs_buf[source].astype(jnp.float32)
        gathered[pl.ds(pl.multiple_of(peer * PIECE, PIECE), PIECE), :] = reduced.astype(jnp.bfloat16)
        for d in range(1, PEERS):
            ag_copy(d).start()
        fin_copy(peer).start()
        for d in range(1, PEERS):
            source = lax.rem(peer + PEERS - d, PEERS)
            ag_arrival(source).wait_recv()
            fin_copy(source).start()

    @pl.when(stays)
    def _():
        for piece in range(PEERS):
            fin_copy(piece).wait_recv()

    clip_out[...] = gathered[...].astype(jnp.float32)

    for way in range(2):
        for hop in range(4):
            for order in range(2):
                if 2 * hop + order < 7:
                    ring_copy(way, hop, order).wait_send()
    for zz in range(ZS):
        for which in range(2):
            sib_copy(zz, which).wait_send()
    for copy in total_copies():
        copy.wait_send()

    @pl.when(stays)
    def _():
        for part in range(3):
            grad_copy(part).wait_send()

    @pl.when(moves)
    def _():
        for copy in swap_copies():
            copy.wait_send()
        loss_copy.wait_send()
        for part in range(3):
            ret_copy(part).wait_send()
        for piece in range(PEERS):
            @pl.when(piece != peer)
            def _():
                rs_copy(piece).wait_send()
            fin_copy(piece).wait_send()
        for d in range(1, PEERS):
            ag_copy(d).wait_send()


def on_device(clip_embed, seg_feats, pair_index):
    bf16, f32, i32 = jnp.bfloat16, jnp.float32, jnp.int32
    vmem = pl.BlockSpec(memory_space=pltpu.VMEM)
    dma = pltpu.SemaphoreType.DMA
    return pl.pallas_call(
        kernel,
        name="ntxent",
        out_shape=(
            jax.ShapeDtypeStruct((1, ROWS), f32),
            jax.ShapeDtypeStruct((1, ROWS, E), f32),
            jax.ShapeDtypeStruct((ROWS, E), f32),
        ),
        in_specs=[vmem] * 3,
        out_specs=(vmem,) * 3,
        scratch_shapes=[
            pltpu.VMEM((ZS, PAIR, E), bf16),
            pltpu.VMEM((ZS, E, PAIR), bf16),
            pltpu.VMEM((ZS, PAIR, ROWS), bf16),
            pltpu.VMEM((ZS, 2, 1, ROWS), f32),
            pltpu.VMEM((E, ROWS), bf16),
            pltpu.VMEM((ROWS, E), bf16),
            pltpu.VMEM((ROWS, E), bf16),
            pltpu.VMEM((ROWS, E), bf16),
            pltpu.VMEM((1, ROWS), i32),
            pltpu.VMEM((1, ROWS), f32),
            pltpu.VMEM((E, ROWS), f32),
            pltpu.VMEM((E, ROWS), f32),
            pltpu.VMEM((E, ROWS), f32),
            pltpu.VMEM((E, ROWS), f32),
            pltpu.VMEM((ROWS, E), bf16),
            pltpu.VMEM((ROWS, E), bf16),
            pltpu.VMEM((ROWS, E), f32),
            pltpu.VMEM((1, ROWS), f32),
            pltpu.VMEM((1, ROWS), f32),
            pltpu.VMEM((ROWS, E), bf16),
            pltpu.VMEM((PEERS, PIECE, E), bf16),
            pltpu.VMEM((ROWS, E), bf16),
            dma((5,)), dma((5,)),
            dma((2, 7)), dma((2, 7)),
            dma((ZS, 2)), dma((ZS, 2)),
            dma((ZS, 2)), dma((ZS, 2)),
            dma((4,)), dma((4,)),
            dma((3,)), dma((3,)),
            dma((PEERS,)), dma((PEERS,)),
            dma((PEERS,)), dma((PEERS,)),
            dma((PEERS,)), dma((PEERS,)),
        ],
        compiler_params=pltpu.CompilerParams(
            collective_id=0, has_side_effects=True, vmem_limit_bytes=56 * 2**20
        ),
    )(clip_embed, seg_feats, pair_index)


def solution(mesh):
    placed = (P("clip", None), P("tm", "clip", None), P("tm", "clip"))
    return jax.shard_map(
        on_device,
        mesh=mesh,
        in_specs=placed,
        out_specs=(P("tm", "clip"), P("tm", "clip", None), P("clip", None)),
        check_vma=False,
    )
```

```python
import math

import jax
import jax.numpy as jnp
from jax import lax
from jax.experimental import pallas as pl
from jax.experimental.pallas import tpu as pltpu
from jax.sharding import PartitionSpec as P

MESH = pl.DeviceIdType.MESH
logit_scale = 14.0
norm_eps = 1e-06
exp2_scale = logit_scale * math.log2(math.e)

RS_DTYPE = jnp.bfloat16
ZS = 8
ROWS = 384
CHUNKS = 4
CHUNK = ROWS // CHUNKS
PAIR = 2 * ROWS
E = 512
PEERS = 8
PARTS = 3
PART = ROWS // PARTS
PIECE = PART // PEERS
RING_COPIES = CHUNKS * 7 // 2


def remote(src, dst, send_sem, recv_sem, device):
    return pltpu.make_async_remote_copy(
        src_ref=src, dst_ref=dst, send_sem=send_sem, recv_sem=recv_sem,
        device_id=device, device_id_type=MESH,
    )


def dot(a, b):
    return jnp.dot(a, b, preferred_element_type=jnp.float32)


def kernel(
    clip_hbm, feat_hbm, pair_hbm,
    loss_out, seg_out, gathered,
    u_all, ut_all, expo_all, columns, tot_all, unit_t, stage, raw_clip, raw_feat, home_clip, home_feat, partner, totals,
    pull_one, pull_pos, acc, summed_t, ret_stage, ret, sib_grad, loss_stage, loss_ret,
    rs_send, rs_buf,
    load_s, swap_s, swap_r, ring_s, ring_r, sib_s, sib_r, tot_s, tot_r, ret_s, ret_r, grad_s, grad_r,
    rs_s, rs_r, ag_s, ag_r, fin_s, fin_r,
):
    clip = lax.axis_index("clip")
    tm = lax.axis_index("tm")
    z, x = clip // 2, lax.rem(clip, 2)
    peer, core = tm // 2, lax.rem(tm, 2)
    stays = x == core
    moves = x != core

    def at(zz, xx, pp, cc):
        return (zz * 2 + xx, pp * 2 + cc)

    def ring(offset):
        return lax.rem(z + offset + ZS, ZS)

    sibling = at(z, x, peer, 1 - core)
    swapped = at(z, 1 - x, peer, 1 - core)

    barrier = pltpu.get_barrier_semaphore()

    def greet(device):
        pl.semaphore_signal(barrier, inc=1, device_id=device, device_id_type=MESH)

    greet(at(ring(1), x, peer, core))
    greet(at(ring(-1), x, peer, core))
    greet(sibling)

    @pl.when(moves)
    def _():
        greet(swapped)
        for d in range(1, PEERS):
            greet(at(z, x, lax.rem(peer + d, PEERS), core))

    loads = [
        pltpu.make_async_copy(clip_hbm, home_clip, load_s.at[0]),
        pltpu.make_async_copy(feat_hbm.at[0], home_feat, load_s.at[1]),
    ]
    pair_load = pltpu.make_async_copy(pair_hbm, partner, load_s.at[2])
    for load in loads:
        load.start()
    for load in loads:
        load.wait()

    summed = home_clip[...].astype(jnp.float32) + home_feat[...].astype(jnp.float32)
    factor = lax.rsqrt(jnp.sum(summed * summed, 1, keepdims=True) + E * norm_eps)
    unit = (summed * factor).astype(jnp.bfloat16)

    def chunk_of(zz, block, which):
        return u_all.at[zz, pl.ds(pl.multiple_of(block * ROWS + which * CHUNK, CHUNK), CHUNK)]

    def swap_unit(which, block):
        return remote(stage.at[pl.ds(which * CHUNK, CHUNK)], chunk_of(z, block, which),
                      swap_s.at[which], swap_r.at[which], swapped)

    def swap_raw():
        return [
            remote(feat_hbm.at[0], raw_feat, swap_s.at[CHUNKS], swap_r.at[CHUNKS], swapped),
            remote(clip_hbm, raw_clip, swap_s.at[CHUNKS + 1], swap_r.at[CHUNKS + 1], swapped),
        ]

    swap_pair = remote(pair_hbm, partner, swap_s.at[CHUNKS + 2], swap_r.at[CHUNKS + 2], swapped)

    def order_chunk(way, order):
        return order if way == 0 else CHUNKS - 1 - order

    def ring_copy(way, hop, order):
        source, target = (ring(-hop), ring(1)) if way == 0 else (ring(hop), ring(-1))
        ref = chunk_of(source, core, order_chunk(way, order))
        index = CHUNKS * hop + order
        return remote(ref, ref, ring_s.at[way, index], ring_r.at[way, index], at(target, x, peer, core))

    def sib_copy(source, which):
        ref = chunk_of(source, core, which)
        return remote(ref, ref, sib_s.at[source, which], sib_r.at[source, which], sibling)

    def sib_arrival(source, which):
        ref = chunk_of(source, 1 - core, which)
        return remote(ref, ref, sib_s.at[source, which], sib_r.at[source, which], sibling)

    swap_order = [c for o in range(CHUNKS // 2) for c in (o, CHUNKS - 1 - o)]

    @pl.when(stays)
    def _():
        pair_load.start()
        u_all[z, pl.ds(pl.multiple_of(core * ROWS, ROWS), ROWS), :] = unit
        pl.semaphore_wait(barrier, 3)
        for order in range(CHUNKS):
            for way in range(2):
                ring_copy(way, 0, order).start()
        for which in swap_order:
            sib_copy(z, which).start()
        raw_clip[...] = home_clip[...]
        raw_feat[...] = home_feat[...]
        pair_load.wait()

    @pl.when(moves)
    def _():
        stage[...] = unit
        pl.semaphore_wait(barrier, 3 + PEERS)
        for which in swap_order:
            swap_unit(which, x).start()
        swap_pair.start()
        for order in range(CHUNKS // 2):
            for which in (order, CHUNKS - 1 - order):
                swap_unit(which, core).wait_recv()
            for way in range(2):
                ring_copy(way, 0, order).start()
            for which in (order, CHUNKS - 1 - order):
                sib_copy(z, which).start()
        for order in range(CHUNKS // 2, CHUNKS):
            for way in range(2):
                ring_copy(way, 0, order).start()
        swap_pair.wait_recv()

    unit_t[...] = u_all[z, pl.ds(pl.multiple_of(core * ROWS, ROWS), ROWS), :].T
    totals[...] = jnp.zeros_like(totals)
    pull_one[...] = jnp.zeros_like(pull_one)
    pull_pos[...] = jnp.zeros_like(pull_pos)

    def column_ids(zz):
        return lax.broadcasted_iota(jnp.int32, (PAIR, ROWS), 0) + zz * PAIR

    def block_of(step):
        hop = (step + 1) // 2
        return ring(jnp.where(lax.rem(step, 2) == 1, -hop, hop))

    def score_part(zz):
        score = dot(u_all[zz], unit_t[...])
        own = lax.broadcasted_iota(jnp.int32, (1, ROWS), 1) + (z * PAIR + core * ROWS)
        expo = jnp.where(column_ids(zz) != own, jnp.exp2(score * exp2_scale - exp2_scale), 0.0)
        totals[...] += jnp.sum(expo, 0, keepdims=True)
        expo_all[zz] = expo.astype(jnp.bfloat16)

    def pull_part(zz):
        ut_all[zz] = u_all[zz].T
        columns[:, :ROWS] = expo_all[zz]
        columns[:, ROWS:] = jnp.where(column_ids(zz) == partner[...], 1.0, 0.0).astype(jnp.bfloat16)
        both = dot(ut_all[zz], columns[...])
        pull_one[...] += both[:, :ROWS]
        pull_pos[...] += both[:, ROWS:]

    def send_on(way, hop, order):
        @pl.when(hop <= (3 if order < CHUNKS // 2 else 2))
        def _():
            ring_copy(way, hop, order).start()

        source = ring(-hop) if way == 0 else ring(hop)
        sib_copy(source, order_chunk(way, order)).start()

    def pass_on(hop, order):
        for way in range(2):
            source = ring(-hop) if way == 0 else ring(hop)
            ref = chunk_of(source, core, order_chunk(way, order))
            index = CHUNKS * (hop - 1) + order
            remote(ref, ref, ring_s.at[way, index], ring_r.at[way, index], sibling).wait_recv()
            send_on(way, hop, order)

    def events(k, part):
        hop = k // 2 + 1
        group = CHUNKS // 4
        for odd in range(2):
            orders = [odd * (CHUNKS // 2) + part * group + i for i in range(group)]

            @pl.when(lax.rem(k, 2) == odd)
            def _():
                for order in orders:
                    pass_on(hop, order)

    def gather_step(step, carry):
        @pl.when(step < 6)
        def _():
            events(step, 0)

        @pl.when(step > 0)
        def _():
            pull_part(block_of(step - 1))

        @pl.when(step < 6)
        def _():
            events(step, 1)

        @pl.when((step == 3) & moves)
        def _():
            for copy in swap_raw():
                copy.start()

        @pl.when(step == 6)
        def _():
            @pl.when(moves)
            def _():
                for copy in swap_raw():
                    copy.wait_recv()

            summed_t[...] = (raw_clip[...].astype(jnp.float32) + raw_feat[...].astype(jnp.float32)).T

        @pl.when(step == 7)
        def _():
            events(step - 1, 0)
            events(step - 1, 1)

        zz = block_of(step)
        for which in range(CHUNKS):
            sib_arrival(zz, which).wait_recv()
        score_part(zz)
        return carry

    lax.fori_loop(0, ZS, gather_step, 0)

    tot_all[z, core] = totals[...]
    others = [(dz, dc) for dz in (4, 3, 5, 2, 6, 1, 7, 0) for dc in range(2) if dz or dc]

    def total_copy(dz, dc):
        ref = tot_all.at[z, core]
        return remote(ref, ref, tot_s.at[dz, dc], tot_r.at[z, core], at(ring(dz), x, peer, lax.rem(core + dc, 2)))

    def total_arrival(zz, block):
        ref = tot_all.at[zz, block]
        return remote(ref, ref, tot_s.at[0, 0], tot_r.at[zz, block], sibling)

    loss_copy = remote(loss_stage, loss_ret, ret_s.at[PARTS], ret_r.at[PARTS], swapped)

    for dz, dc in others:
        total_copy(dz, dc).start()
    pull_part(block_of(ZS - 1))

    inverse = 1.0 / totals[...]
    positive = jnp.sum(unit_t[...].astype(jnp.float32) * pull_pos[...], 0, keepdims=True)
    loss = logit_scale * (1.0 - positive) + jnp.log(totals[...])

    @pl.when(stays)
    def _():
        loss_out[...] = loss

    @pl.when(moves)
    def _():
        loss_stage[...] = loss
        loss_copy.start()
    acc[...] = inverse * pull_one[...] - 2.0 * pull_pos[...]
    factor_t = lax.rsqrt(jnp.sum(summed_t[...] * summed_t[...], 0, keepdims=True) + E * norm_eps)

    def second(zz, own):
        if not own:
            total_arrival(zz, core).wait_recv()
        total_arrival(zz, 1 - core).wait_recv()
        scale = 1.0 / jnp.concatenate([tot_all[zz, 0], tot_all[zz, 1]], 1)
        scaled = (ut_all[zz].astype(jnp.float32) * scale).astype(jnp.bfloat16)
        return dot(scaled, expo_all[zz])

    def second_hop(hop, carry):
        acc[...] += second(ring(-hop), False) + second(ring(hop), False)
        return carry

    acc[...] += second(z, True)
    lax.fori_loop(1, 4, second_hop, 0)
    acc[...] += second(ring(4), False)

    def part_rows(part):
        return slice(part * PART, (part + 1) * PART)

    def ret_copy(part):
        rows = pl.ds(part * PART, PART)
        return remote(ret_stage.at[rows], ret.at[rows], ret_s.at[part], ret_r.at[part], swapped)

    def grad_copy(part):
        rows = pl.ds(part * PART, PART)
        return remote(seg_out.at[0, rows], sib_grad.at[rows], grad_s.at[part], grad_r.at[part], sibling)

    for part in range(PARTS):
        rows = part_rows(part)
        grad_unit = logit_scale * acc[:, rows]
        summed_part = summed_t[:, rows]
        factor_part = factor_t[:, rows]
        along = jnp.sum(summed_part * grad_unit, 0, keepdims=True)
        grad = (factor_part * grad_unit - factor_part**3 * along * summed_part).T

        @pl.when(stays)
        def _():
            seg_out[0, rows, :] = grad
            grad_copy(part).start()

        @pl.when(moves)
        def _():
            ret_stage[rows, :] = grad.astype(jnp.bfloat16)
            ret_copy(part).start()

    def rs_copy(part, d):
        owner = lax.rem(peer + d, PEERS)
        rows = pl.ds(pl.multiple_of(part * PART + owner * PIECE, PIECE), PIECE)
        return remote(rs_send.at[rows], rs_buf.at[part, peer], rs_s.at[part, d], rs_r.at[part, peer],
                      at(z, x, owner, core))

    def rs_arrival(part, d):
        source = lax.rem(peer + d, PEERS)
        ref = rs_buf.at[part, source]
        return remote(ref, ref, rs_s.at[part, d], rs_r.at[part, source], sibling)

    def gathered_rows(part, owner):
        return gathered.at[pl.ds(pl.multiple_of(part * PART + owner * PIECE, PIECE), PIECE)]

    def ag_copy(part, d):
        ref = gathered_rows(part, peer)
        return remote(ref, ref, ag_s.at[part, d], ag_r.at[part, peer], at(z, x, lax.rem(peer + d, PEERS), core))

    def ag_arrival(part, source):
        ref = gathered_rows(part, source)
        return remote(ref, ref, ag_s.at[part, 0], ag_r.at[part, source], sibling)

    def fin_copy(part):
        ref = gathered.at[pl.ds(part * PART, PART)]
        return remote(ref, ref, fin_s.at[part], fin_r.at[part], sibling)

    @pl.when(moves)
    def _():
        loss_copy.wait_recv()
        loss_out[...] = loss_ret[...]
        for part in range(PARTS):
            rows = part_rows(part)
            ret_copy(part).wait_recv()
            grad_copy(part).wait_recv()
            home = ret[rows, :].astype(jnp.float32)
            seg_out[0, rows, :] = home
            rs_send[rows, :] = (home + sib_grad[rows, :]).astype(RS_DTYPE)
            for d in (4, 3, 5, 2, 6, 1, 7):
                rs_copy(part, d).start()
            rs_buf[part, peer] = rs_send[pl.ds(pl.multiple_of(part * PART + peer * PIECE, PIECE), PIECE), :]
        for part in range(PARTS):
            for d in range(1, PEERS):
                rs_arrival(part, d).wait_recv()
            reduced = rs_buf[part, 0].astype(jnp.float32)
            for source in range(1, PEERS):
                reduced += rs_buf[part, source].astype(jnp.float32)
            gathered[pl.ds(pl.multiple_of(part * PART + peer * PIECE, PIECE), PIECE), :] = reduced.astype(jnp.bfloat16)
            for d in (4, 3, 5, 2, 6, 1, 7):
                ag_copy(part, d).start()
        for part in range(PARTS):
            for d in (1, 7, 2, 6, 3, 5, 4):
                source = lax.rem(peer + PEERS - d, PEERS)
                ag_arrival(part, source).wait_recv()
            fin_copy(part).start()

    @pl.when(stays)
    def _():
        for part in range(PARTS):
            fin_copy(part).wait_recv()

    for way in range(2):
        for index in range(RING_COPIES):
            ring_copy(way, index // CHUNKS, index % CHUNKS).wait_send()
    for zz in range(ZS):
        for which in range(CHUNKS):
            sib_copy(zz, which).wait_send()
    for dz, dc in others:
        total_copy(dz, dc).wait_send()

    @pl.when(stays)
    def _():
        for part in range(PARTS):
            grad_copy(part).wait_send()

    @pl.when(moves)
    def _():
        for which in range(CHUNKS):
            swap_unit(which, x).wait_send()
        swap_pair.wait_send()
        for copy in swap_raw():
            copy.wait_send()
        loss_copy.wait_send()
        for part in range(PARTS):
            ret_copy(part).wait_send()
            for d in range(1, PEERS):
                rs_copy(part, d).wait_send()
            for d in range(1, PEERS):
                ag_copy(part, d).wait_send()
            fin_copy(part).wait_send()


def hand_over(loss_in, seg_in, sum_in, loss_out, seg_out, clip_out, wide, sems):
    copies = [
        pltpu.make_async_copy(seg_in, seg_out, sems.at[0]),
        pltpu.make_async_copy(loss_in, loss_out, sems.at[1]),
        pltpu.make_async_copy(wide, clip_out, sems.at[2]),
    ]
    for copy in copies[:2]:
        copy.start()
    wide[...] = sum_in[...].astype(jnp.float32)
    copies[2].start()
    for copy in copies:
        copy.wait()


def on_device(clip_embed, seg_feats, pair_index):
    bf16, f32, i32 = jnp.bfloat16, jnp.float32, jnp.int32
    vmem = pl.BlockSpec(memory_space=pltpu.VMEM)
    anywhere = pl.BlockSpec(memory_space=pl.ANY)
    hbm = pl.BlockSpec(memory_space=pltpu.HBM)
    dma = pltpu.SemaphoreType.DMA
    loss, seg, total = pl.pallas_call(
        kernel,
        name="ntxent",
        out_shape=(
            pltpu.VMEM((1, ROWS), f32),
            pltpu.VMEM((1, ROWS, E), f32),
            pltpu.VMEM((ROWS, E), bf16),
        ),
        in_specs=[hbm] * 3,
        out_specs=(vmem,) * 3,
        scratch_shapes=[
            pltpu.VMEM((ZS, PAIR, E), bf16),
            pltpu.VMEM((ZS, E, PAIR), bf16),
            pltpu.VMEM((ZS, PAIR, ROWS), bf16),
            pltpu.VMEM((PAIR, 2 * ROWS), bf16),
            pltpu.VMEM((ZS, 2, 1, ROWS), f32),
            pltpu.VMEM((E, ROWS), bf16),
            pltpu.VMEM((ROWS, E), bf16),
            pltpu.VMEM((ROWS, E), bf16),
            pltpu.VMEM((ROWS, E), bf16),
            pltpu.VMEM((ROWS, E), bf16),
            pltpu.VMEM((ROWS, E), bf16),
            pltpu.VMEM((1, ROWS), i32),
            pltpu.VMEM((1, ROWS), f32),
            pltpu.VMEM((E, ROWS), f32),
            pltpu.VMEM((E, ROWS), f32),
            pltpu.VMEM((E, ROWS), f32),
            pltpu.VMEM((E, ROWS), f32),
            pltpu.VMEM((ROWS, E), bf16),
            pltpu.VMEM((ROWS, E), bf16),
            pltpu.VMEM((ROWS, E), f32),
            pltpu.VMEM((1, ROWS), f32),
            pltpu.VMEM((1, ROWS), f32),
            pltpu.VMEM((ROWS, E), RS_DTYPE),
            pltpu.VMEM((PARTS, PEERS, PIECE, E), RS_DTYPE),
            dma((3,)),
            dma((CHUNKS + 3,)), dma((CHUNKS + 3,)),
            dma((2, RING_COPIES)), dma((2, RING_COPIES)),
            dma((ZS, CHUNKS)), dma((ZS, CHUNKS)),
            dma((ZS, 2)), dma((ZS, 2)),
            dma((PARTS + 1,)), dma((PARTS + 1,)),
            dma((PARTS,)), dma((PARTS,)),
            dma((PARTS, PEERS)), dma((PARTS, PEERS)),
            dma((PARTS, PEERS)), dma((PARTS, PEERS)),
            dma((PARTS,)), dma((PARTS,)),
        ],
        compiler_params=pltpu.CompilerParams(
            collective_id=0, has_side_effects=True, vmem_limit_bytes=56 * 2**20
        ),
    )(clip_embed, seg_feats, pair_index)
    return pl.pallas_call(
        hand_over,
        name="hand_over",
        out_shape=(
            jax.ShapeDtypeStruct((1, ROWS), f32),
            jax.ShapeDtypeStruct((1, ROWS, E), f32),
            jax.ShapeDtypeStruct((ROWS, E), f32),
        ),
        in_specs=[vmem] * 3,
        out_specs=(anywhere,) * 3,
        scratch_shapes=[pltpu.VMEM((ROWS, E), f32), dma((3,))],
        compiler_params=pltpu.CompilerParams(vmem_limit_bytes=4 * 2**20),
    )(loss, seg, total)


def solution(mesh):
    placed = (P("clip", None), P("tm", "clip", None), P("tm", "clip"))
    return jax.shard_map(
        on_device,
        mesh=mesh,
        in_specs=placed,
        out_specs=(P("tm", "clip"), P("tm", "clip", None), P("clip", None)),
        check_vma=False,
    )
```

```python
import math

import jax
import jax.numpy as jnp
from jax import lax
from jax.experimental import pallas as pl
from jax.experimental.pallas import tpu as pltpu
from jax.sharding import PartitionSpec as P

MESH = pl.DeviceIdType.MESH
logit_scale = 14.0
norm_eps = 1e-06
exp2_scale = logit_scale * math.log2(math.e)

RS_DTYPE = jnp.bfloat16
ZS = 8
ROWS = 384
CHUNKS = 4
CHUNK = ROWS // CHUNKS
PAIR = 2 * ROWS
E = 512
PEERS = 8
PARTS = 3
PART = ROWS // PARTS
PIECE = PART // PEERS
RING_COPIES = CHUNKS * 7 // 2


def remote(src, dst, send_sem, recv_sem, device):
    return pltpu.make_async_remote_copy(
        src_ref=src, dst_ref=dst, send_sem=send_sem, recv_sem=recv_sem,
        device_id=device, device_id_type=MESH,
    )


def dot(a, b):
    return jnp.dot(a, b, preferred_element_type=jnp.float32)


def kernel(
    clip_hbm, feat_hbm, pair_hbm,
    loss_out, seg_out, gathered,
    u_all, ut_all, expo_all, columns, tot_all, unit_t, stage, raw_clip, raw_feat, home_clip, home_feat, partner, totals,
    pull_one, pull_pos, acc, summed_t, ret_stage, ret, sib_grad, loss_stage, loss_ret,
    rs_send, rs_buf,
    load_s, swap_s, swap_r, ring_s, ring_r, sib_s, sib_r, tot_s, tot_r, ret_s, ret_r, grad_s, grad_r,
    rs_s, rs_r, ag_s, ag_r, fin_s, fin_r, near, go,
):
    clip = lax.axis_index("clip")
    tm = lax.axis_index("tm")
    z, x = clip // 2, lax.rem(clip, 2)
    peer, core = tm // 2, lax.rem(tm, 2)
    stays = x == core
    moves = x != core

    def at(zz, xx, pp, cc):
        return (zz * 2 + xx, pp * 2 + cc)

    def ring(offset):
        return lax.rem(z + offset + ZS, ZS)

    sibling = at(z, x, peer, 1 - core)
    swapped = at(z, 1 - x, peer, 1 - core)

    barrier = pltpu.get_barrier_semaphore()

    def greet(device, semaphore):
        pl.semaphore_signal(semaphore, inc=1, device_id=device, device_id_type=MESH)

    neighbours = [at(ring(1), x, peer, core), at(ring(-1), x, peer, core), swapped]

    @pl.when(stays)
    def _():
        for device in neighbours:
            greet(device, barrier)

    @pl.when(moves)
    def _():
        greet(sibling, barrier)
        for d in range(1, PEERS):
            greet(at(z, x, lax.rem(peer + d, PEERS), core), barrier)

    loads = [
        pltpu.make_async_copy(clip_hbm, home_clip, load_s.at[0]),
        pltpu.make_async_copy(feat_hbm.at[0], home_feat, load_s.at[1]),
    ]
    pair_load = pltpu.make_async_copy(pair_hbm, partner, load_s.at[2])
    for load in loads:
        load.start()
    for load in loads:
        load.wait()

    summed = home_clip[...].astype(jnp.float32) + home_feat[...].astype(jnp.float32)
    factor = lax.rsqrt(jnp.sum(summed * summed, 1, keepdims=True) + E * norm_eps)
    unit = (summed * factor).astype(jnp.bfloat16)

    def chunk_of(zz, block, which):
        return u_all.at[zz, pl.ds(pl.multiple_of(block * ROWS + which * CHUNK, CHUNK), CHUNK)]

    def swap_unit(which, block):
        return remote(stage.at[pl.ds(which * CHUNK, CHUNK)], chunk_of(z, block, which),
                      swap_s.at[which], swap_r.at[which], swapped)

    def swap_raw():
        return [
            remote(feat_hbm.at[0], raw_feat, swap_s.at[CHUNKS], swap_r.at[CHUNKS], swapped),
            remote(clip_hbm, raw_clip, swap_s.at[CHUNKS + 1], swap_r.at[CHUNKS + 1], swapped),
        ]

    swap_pair = remote(pair_hbm, partner, swap_s.at[CHUNKS + 2], swap_r.at[CHUNKS + 2], swapped)

    def order_chunk(way, order):
        return order if way == 0 else CHUNKS - 1 - order

    def ring_copy(way, hop, order):
        source, target = (ring(-hop), ring(1)) if way == 0 else (ring(hop), ring(-1))
        ref = chunk_of(source, core, order_chunk(way, order))
        index = CHUNKS * hop + order
        return remote(ref, ref, ring_s.at[way, index], ring_r.at[way, index], at(target, x, peer, core))

    def sib_copy(source, which):
        ref = chunk_of(source, core, which)
        return remote(ref, ref, sib_s.at[source, which], sib_r.at[source, which], sibling)

    def sib_arrival(source, which):
        ref = chunk_of(source, 1 - core, which)
        return remote(ref, ref, sib_s.at[source, which], sib_r.at[source, which], sibling)

    swap_order = [c for o in range(CHUNKS // 2) for c in (o, CHUNKS - 1 - o)]

    @pl.when(stays)
    def _():
        pair_load.start()
        u_all[z, pl.ds(pl.multiple_of(core * ROWS, ROWS), ROWS), :] = unit
        pl.semaphore_wait(barrier, 4)
        for device in neighbours:
            greet(device, near)
        for order in range(CHUNKS):
            for way in range(2):
                ring_copy(way, 0, order).start()
        for which in swap_order:
            sib_copy(z, which).start()
        pl.semaphore_wait(near, 3)
        greet(sibling, go)
        raw_clip[...] = home_clip[...]
        raw_feat[...] = home_feat[...]
        pair_load.wait()

    @pl.when(moves)
    def _():
        stage[...] = unit
        pl.semaphore_wait(go, 1)
        for which in swap_order:
            swap_unit(which, x).start()
        swap_pair.start()
        for order in range(CHUNKS // 2):
            for which in (order, CHUNKS - 1 - order):
                swap_unit(which, core).wait_recv()
            for way in range(2):
                ring_copy(way, 0, order).start()
            for which in (order, CHUNKS - 1 - order):
                sib_copy(z, which).start()
        for order in range(CHUNKS // 2, CHUNKS):
            for way in range(2):
                ring_copy(way, 0, order).start()
        swap_pair.wait_recv()

    unit_t[...] = u_all[z, pl.ds(pl.multiple_of(core * ROWS, ROWS), ROWS), :].T
    totals[...] = jnp.zeros_like(totals)
    pull_one[...] = jnp.zeros_like(pull_one)
    pull_pos[...] = jnp.zeros_like(pull_pos)

    def column_ids(zz):
        return lax.broadcasted_iota(jnp.int32, (PAIR, ROWS), 0) + zz * PAIR

    def block_of(step):
        hop = (step + 1) // 2
        return ring(jnp.where(lax.rem(step, 2) == 1, -hop, hop))

    def score_part(zz):
        score = dot(u_all[zz], unit_t[...])
        own = lax.broadcasted_iota(jnp.int32, (1, ROWS), 1) + (z * PAIR + core * ROWS)
        expo = jnp.where(column_ids(zz) != own, jnp.exp2(score * exp2_scale - exp2_scale), 0.0)
        totals[...] += jnp.sum(expo, 0, keepdims=True)
        expo_all[zz] = expo.astype(jnp.bfloat16)

    def pull_part(zz):
        ut_all[zz] = u_all[zz].T
        columns[:, :ROWS] = expo_all[zz]
        columns[:, ROWS:] = jnp.where(column_ids(zz) == partner[...], 1.0, 0.0).astype(jnp.bfloat16)
        both = dot(ut_all[zz], columns[...])
        pull_one[...] += both[:, :ROWS]
        pull_pos[...] += both[:, ROWS:]

    def send_on(way, hop, order):
        @pl.when(hop <= (3 if order < CHUNKS // 2 else 2))
        def _():
            ring_copy(way, hop, order).start()

        source = ring(-hop) if way == 0 else ring(hop)
        sib_copy(source, order_chunk(way, order)).start()

    def pass_on(hop, order):
        for way in range(2):
            source = ring(-hop) if way == 0 else ring(hop)
            ref = chunk_of(source, core, order_chunk(way, order))
            index = CHUNKS * (hop - 1) + order
            remote(ref, ref, ring_s.at[way, index], ring_r.at[way, index], sibling).wait_recv()
            send_on(way, hop, order)

    def events(k, part):
        hop = k // 2 + 1
        group = CHUNKS // 4
        for odd in range(2):
            orders = [odd * (CHUNKS // 2) + part * group + i for i in range(group)]

            @pl.when(lax.rem(k, 2) == odd)
            def _():
                for order in orders:
                    pass_on(hop, order)

    def gather_step(step, carry):
        group = jnp.minimum(step, 6)

        @pl.when(step != 6)
        def _():
            events(group, 0)

        @pl.when(step > 0)
        def _():
            pull_part(block_of(step - 1))

        @pl.when(step != 6)
        def _():
            events(group, 1)

        @pl.when((step == 3) & moves)
        def _():
            for copy in swap_raw():
                copy.start()

        @pl.when(step == 6)
        def _():
            @pl.when(moves)
            def _():
                for copy in swap_raw():
                    copy.wait_recv()

            summed_t[...] = (raw_clip[...].astype(jnp.float32) + raw_feat[...].astype(jnp.float32)).T

        zz = block_of(step)
        for which in range(CHUNKS):
            sib_arrival(zz, which).wait_recv()
        score_part(zz)
        return carry

    lax.fori_loop(0, ZS, gather_step, 0)

    tot_all[z, core] = totals[...]
    others = [(dz, dc) for dz in (4, 3, 5, 2, 6, 1, 7, 0) for dc in range(2) if dz or dc]

    def total_copy(dz, dc):
        ref = tot_all.at[z, core]
        return remote(ref, ref, tot_s.at[dz, dc], tot_r.at[z, core], at(ring(dz), x, peer, lax.rem(core + dc, 2)))

    def total_arrival(zz, block):
        ref = tot_all.at[zz, block]
        return remote(ref, ref, tot_s.at[0, 0], tot_r.at[zz, block], sibling)

    loss_copy = remote(loss_stage, loss_ret, ret_s.at[PARTS], ret_r.at[PARTS], swapped)

    for dz, dc in others:
        total_copy(dz, dc).start()
    pull_part(block_of(ZS - 1))

    inverse = 1.0 / totals[...]
    positive = jnp.sum(unit_t[...].astype(jnp.float32) * pull_pos[...], 0, keepdims=True)
    loss = logit_scale * (1.0 - positive) + jnp.log(totals[...])

    @pl.when(stays)
    def _():
        loss_out[...] = loss

    @pl.when(moves)
    def _():
        loss_stage[...] = loss
        loss_copy.start()
    acc[...] = inverse * pull_one[...] - 2.0 * pull_pos[...]
    factor_t = lax.rsqrt(jnp.sum(summed_t[...] * summed_t[...], 0, keepdims=True) + E * norm_eps)

    def second(zz, own):
        if not own:
            total_arrival(zz, core).wait_recv()
        total_arrival(zz, 1 - core).wait_recv()
        scale = 1.0 / jnp.concatenate([tot_all[zz, 0], tot_all[zz, 1]], 1)
        scaled = (ut_all[zz].astype(jnp.float32) * scale).astype(jnp.bfloat16)
        return dot(scaled, expo_all[zz])

    def second_hop(hop, carry):
        acc[...] += second(ring(-hop), False) + second(ring(hop), False)
        return carry

    acc[...] += second(z, True)
    lax.fori_loop(1, 4, second_hop, 0)
    acc[...] += second(ring(4), False)

    def part_rows(part):
        return slice(part * PART, (part + 1) * PART)

    def ret_copy(part):
        rows = pl.ds(part * PART, PART)
        return remote(ret_stage.at[rows], ret.at[rows], ret_s.at[part], ret_r.at[part], swapped)

    def grad_copy(part):
        rows = pl.ds(part * PART, PART)
        return remote(seg_out.at[0, rows], sib_grad.at[rows], grad_s.at[part], grad_r.at[part], sibling)

    for part in range(PARTS):
        rows = part_rows(part)
        grad_unit = logit_scale * acc[:, rows]
        summed_part = summed_t[:, rows]
        factor_part = factor_t[:, rows]
        along = jnp.sum(summed_part * grad_unit, 0, keepdims=True)
        grad = (factor_part * grad_unit - factor_part**3 * along * summed_part).T

        @pl.when(stays)
        def _():
            seg_out[0, rows, :] = grad
            grad_copy(part).start()

        @pl.when(moves)
        def _():
            ret_stage[rows, :] = grad.astype(jnp.bfloat16)
            ret_copy(part).start()

    def rs_copy(part, d):
        owner = lax.rem(peer + d, PEERS)
        rows = pl.ds(pl.multiple_of(part * PART + owner * PIECE, PIECE), PIECE)
        return remote(rs_send.at[rows], rs_buf.at[part, peer], rs_s.at[part, d], rs_r.at[part, peer],
                      at(z, x, owner, core))

    def rs_arrival(part, d):
        source = lax.rem(peer + d, PEERS)
        ref = rs_buf.at[part, source]
        return remote(ref, ref, rs_s.at[part, d], rs_r.at[part, source], sibling)

    def gathered_rows(part, owner):
        return gathered.at[pl.ds(pl.multiple_of(part * PART + owner * PIECE, PIECE), PIECE)]

    def ag_copy(part, d):
        ref = gathered_rows(part, peer)
        return remote(ref, ref, ag_s.at[part, d], ag_r.at[part, peer], at(z, x, lax.rem(peer + d, PEERS), core))

    def ag_arrival(part, source):
        ref = gathered_rows(part, source)
        return remote(ref, ref, ag_s.at[part, 0], ag_r.at[part, source], sibling)

    def fin_copy(part):
        ref = gathered.at[pl.ds(part * PART, PART)]
        return remote(ref, ref, fin_s.at[part], fin_r.at[part], sibling)

    @pl.when(moves)
    def _():
        pl.semaphore_wait(barrier, PEERS - 1)
        loss_copy.wait_recv()
        loss_out[...] = loss_ret[...]
        for part in range(PARTS):
            rows = part_rows(part)
            ret_copy(part).wait_recv()
            grad_copy(part).wait_recv()
            home = ret[rows, :].astype(jnp.float32)
            seg_out[0, rows, :] = home
            rs_send[rows, :] = (home + sib_grad[rows, :]).astype(RS_DTYPE)
            for d in (4, 3, 5, 2, 6, 1, 7):
                rs_copy(part, d).start()
            rs_buf[part, peer] = rs_send[pl.ds(pl.multiple_of(part * PART + peer * PIECE, PIECE), PIECE), :]
        for part in range(PARTS):
            for d in range(1, PEERS):
                rs_arrival(part, d).wait_recv()
            reduced = rs_buf[part, 0].astype(jnp.float32)
            for source in range(1, PEERS):
                reduced += rs_buf[part, source].astype(jnp.float32)
            gathered[pl.ds(pl.multiple_of(part * PART + peer * PIECE, PIECE), PIECE), :] = reduced.astype(jnp.bfloat16)
            for d in (4, 3, 5, 2, 6, 1, 7):
                ag_copy(part, d).start()
        for part in range(PARTS):
            for d in (1, 7, 2, 6, 3, 5, 4):
                source = lax.rem(peer + PEERS - d, PEERS)
                ag_arrival(part, source).wait_recv()
            fin_copy(part).start()

    @pl.when(stays)
    def _():
        for part in range(PARTS):
            fin_copy(part).wait_recv()

    for way in range(2):
        for index in range(RING_COPIES):
            ring_copy(way, index // CHUNKS, index % CHUNKS).wait_send()
    for zz in range(ZS):
        for which in range(CHUNKS):
            sib_copy(zz, which).wait_send()
    for dz, dc in others:
        total_copy(dz, dc).wait_send()

    @pl.when(stays)
    def _():
        for part in range(PARTS):
            grad_copy(part).wait_send()

    @pl.when(moves)
    def _():
        for which in range(CHUNKS):
            swap_unit(which, x).wait_send()
        swap_pair.wait_send()
        for copy in swap_raw():
            copy.wait_send()
        loss_copy.wait_send()
        for part in range(PARTS):
            ret_copy(part).wait_send()
            for d in range(1, PEERS):
                rs_copy(part, d).wait_send()
            for d in range(1, PEERS):
                ag_copy(part, d).wait_send()
            fin_copy(part).wait_send()


def hand_over(loss_in, seg_in, sum_in, loss_out, seg_out, clip_out, wide, sems):
    copies = [
        pltpu.make_async_copy(seg_in, seg_out, sems.at[0]),
        pltpu.make_async_copy(loss_in, loss_out, sems.at[1]),
        pltpu.make_async_copy(wide, clip_out, sems.at[2]),
    ]
    for copy in copies[:2]:
        copy.start()
    wide[...] = sum_in[...].astype(jnp.float32)
    copies[2].start()
    for copy in copies:
        copy.wait()


def on_device(clip_embed, seg_feats, pair_index):
    bf16, f32, i32 = jnp.bfloat16, jnp.float32, jnp.int32
    vmem = pl.BlockSpec(memory_space=pltpu.VMEM)
    anywhere = pl.BlockSpec(memory_space=pl.ANY)
    hbm = pl.BlockSpec(memory_space=pltpu.HBM)
    dma = pltpu.SemaphoreType.DMA
    loss, seg, total = pl.pallas_call(
        kernel,
        name="ntxent",
        out_shape=(
            pltpu.VMEM((1, ROWS), f32),
            pltpu.VMEM((1, ROWS, E), f32),
            pltpu.VMEM((ROWS, E), bf16),
        ),
        in_specs=[hbm] * 3,
        out_specs=(vmem,) * 3,
        scratch_shapes=[
            pltpu.VMEM((ZS, PAIR, E), bf16),
            pltpu.VMEM((ZS, E, PAIR), bf16),
            pltpu.VMEM((ZS, PAIR, ROWS), bf16),
            pltpu.VMEM((PAIR, 2 * ROWS), bf16),
            pltpu.VMEM((ZS, 2, 1, ROWS), f32),
            pltpu.VMEM((E, ROWS), bf16),
            pltpu.VMEM((ROWS, E), bf16),
            pltpu.VMEM((ROWS, E), bf16),
            pltpu.VMEM((ROWS, E), bf16),
            pltpu.VMEM((ROWS, E), bf16),
            pltpu.VMEM((ROWS, E), bf16),
            pltpu.VMEM((1, ROWS), i32),
            pltpu.VMEM((1, ROWS), f32),
            pltpu.VMEM((E, ROWS), f32),
            pltpu.VMEM((E, ROWS), f32),
            pltpu.VMEM((E, ROWS), f32),
            pltpu.VMEM((E, ROWS), f32),
            pltpu.VMEM((ROWS, E), bf16),
            pltpu.VMEM((ROWS, E), bf16),
            pltpu.VMEM((ROWS, E), f32),
            pltpu.VMEM((1, ROWS), f32),
            pltpu.VMEM((1, ROWS), f32),
            pltpu.VMEM((ROWS, E), RS_DTYPE),
            pltpu.VMEM((PARTS, PEERS, PIECE, E), RS_DTYPE),
            dma((3,)),
            dma((CHUNKS + 3,)), dma((CHUNKS + 3,)),
            dma((2, RING_COPIES)), dma((2, RING_COPIES)),
            dma((ZS, CHUNKS)), dma((ZS, CHUNKS)),
            dma((ZS, 2)), dma((ZS, 2)),
            dma((PARTS + 1,)), dma((PARTS + 1,)),
            dma((PARTS,)), dma((PARTS,)),
            dma((PARTS, PEERS)), dma((PARTS, PEERS)),
            dma((PARTS, PEERS)), dma((PARTS, PEERS)),
            dma((PARTS,)), dma((PARTS,)),
            pltpu.SemaphoreType.REGULAR, pltpu.SemaphoreType.REGULAR,
        ],
        compiler_params=pltpu.CompilerParams(
            collective_id=0, has_side_effects=True, vmem_limit_bytes=56 * 2**20
        ),
    )(clip_embed, seg_feats, pair_index)
    return pl.pallas_call(
        hand_over,
        name="hand_over",
        out_shape=(
            jax.ShapeDtypeStruct((1, ROWS), f32),
            jax.ShapeDtypeStruct((1, ROWS, E), f32),
            jax.ShapeDtypeStruct((ROWS, E), f32),
        ),
        in_specs=[vmem] * 3,
        out_specs=(anywhere,) * 3,
        scratch_shapes=[pltpu.VMEM((ROWS, E), f32), dma((3,))],
        compiler_params=pltpu.CompilerParams(vmem_limit_bytes=4 * 2**20),
    )(loss, seg, total)


def solution(mesh):
    placed = (P("clip", None), P("tm", "clip", None), P("tm", "clip"))
    return jax.shard_map(
        on_device,
        mesh=mesh,
        in_specs=placed,
        out_specs=(P("tm", "clip"), P("tm", "clip", None), P("clip", None)),
        check_vma=False,
    )
```

```python
import math

import jax
import jax.numpy as jnp
from jax import lax
from jax.experimental import pallas as pl
from jax.experimental.pallas import tpu as pltpu
from jax.sharding import PartitionSpec as P

MESH = pl.DeviceIdType.MESH
logit_scale = 14.0
norm_eps = 1e-06
exp2_scale = logit_scale * math.log2(math.e)

ZS = 8
ROWS = 384
CHUNKS = 4
CHUNK = ROWS // CHUNKS
PAIR = 2 * ROWS
E = 512
PEERS = 8
PARTS = 3
PART = ROWS // PARTS
PIECE = PART // PEERS
RING_COPIES = CHUNKS * 7 // 2


def remote(src, dst, send_sem, recv_sem, device):
    return pltpu.make_async_remote_copy(
        src_ref=src, dst_ref=dst, send_sem=send_sem, recv_sem=recv_sem,
        device_id=device, device_id_type=MESH,
    )


def dot(a, b):
    return jnp.dot(a, b, preferred_element_type=jnp.float32)


def kernel(
    clip_hbm, feat_hbm, pair_hbm,
    loss_out, seg_out, gathered,
    u_all, ut_all, expo_all, columns, scaled_last, tot_all, unit_t, stage, raw_clip, raw_feat, home_clip, home_feat, partner, totals,
    pull_one, pull_pos, acc, summed_t, ret_stage, ret, loss_stage, loss_ret,
    rs_buf,
    load_s, swap_s, swap_r, ring_s, ring_r, sib_s, sib_r, tot_s, tot_r, ret_s, ret_r,
    rs_s, rs_r, ag_s, ag_r, fin_s, fin_r, near, go, peers_in,
):
    clip = lax.axis_index("clip")
    tm = lax.axis_index("tm")
    z, x = clip // 2, lax.rem(clip, 2)
    peer, core = tm // 2, lax.rem(tm, 2)
    stays = x == core
    moves = x != core

    def at(zz, xx, pp, cc):
        return (zz * 2 + xx, pp * 2 + cc)

    def ring(offset):
        return lax.rem(z + offset + ZS, ZS)

    sibling = at(z, x, peer, 1 - core)
    swapped = at(z, 1 - x, peer, 1 - core)

    barrier = pltpu.get_barrier_semaphore()

    def greet(device, semaphore):
        pl.semaphore_signal(semaphore, inc=1, device_id=device, device_id_type=MESH)

    neighbours = [at(ring(1), x, peer, core), at(ring(-1), x, peer, core), swapped]

    @pl.when(stays)
    def _():
        for device in neighbours:
            greet(device, barrier)
        for d in range(PEERS):
            greet(at(z, 1 - x, lax.rem(peer + d, PEERS), core), barrier)

    @pl.when(moves)
    def _():
        greet(sibling, barrier)

    loads = [
        pltpu.make_async_copy(clip_hbm, home_clip, load_s.at[0]),
        pltpu.make_async_copy(feat_hbm.at[0], home_feat, load_s.at[1]),
    ]
    pair_load = pltpu.make_async_copy(pair_hbm, partner, load_s.at[2])
    for load in loads:
        load.start()
    for load in loads:
        load.wait()

    summed = home_clip[...].astype(jnp.float32) + home_feat[...].astype(jnp.float32)
    factor = lax.rsqrt(jnp.sum(summed * summed, 1, keepdims=True) + E * norm_eps)
    unit = (summed * factor).astype(jnp.bfloat16)

    def chunk_of(zz, block, which):
        return u_all.at[zz, pl.ds(pl.multiple_of(block * ROWS + which * CHUNK, CHUNK), CHUNK)]

    def swap_unit(which, block):
        return remote(stage.at[pl.ds(which * CHUNK, CHUNK)], chunk_of(z, block, which),
                      swap_s.at[which], swap_r.at[which], swapped)

    def swap_raw():
        return [
            remote(feat_hbm.at[0], raw_feat, swap_s.at[CHUNKS], swap_r.at[CHUNKS], swapped),
            remote(clip_hbm, raw_clip, swap_s.at[CHUNKS + 1], swap_r.at[CHUNKS + 1], swapped),
        ]

    swap_pair = remote(pair_hbm, partner, swap_s.at[CHUNKS + 2], swap_r.at[CHUNKS + 2], swapped)

    def order_chunk(way, order):
        return order if way == 0 else CHUNKS - 1 - order

    def ring_copy(way, hop, order):
        source, target = (ring(-hop), ring(1)) if way == 0 else (ring(hop), ring(-1))
        ref = chunk_of(source, core, order_chunk(way, order))
        index = CHUNKS * hop + order
        return remote(ref, ref, ring_s.at[way, index], ring_r.at[way, index], at(target, x, peer, core))

    def sib_copy(source, which):
        ref = chunk_of(source, core, which)
        return remote(ref, ref, sib_s.at[source, which], sib_r.at[source, which], sibling)

    def sib_arrival(source, which):
        ref = chunk_of(source, 1 - core, which)
        return remote(ref, ref, sib_s.at[source, which], sib_r.at[source, which], sibling)

    swap_order = [c for o in range(CHUNKS // 2) for c in (o, CHUNKS - 1 - o)]

    @pl.when(stays)
    def _():
        pair_load.start()
        u_all[z, pl.ds(pl.multiple_of(core * ROWS, ROWS), ROWS), :] = unit
        pl.semaphore_wait(barrier, 4)
        for device in neighbours:
            greet(device, near)
        for order in range(CHUNKS):
            for way in range(2):
                ring_copy(way, 0, order).start()
        for which in swap_order:
            sib_copy(z, which).start()
        pl.semaphore_wait(near, 3)
        greet(sibling, go)
        raw_clip[...] = home_clip[...]
        raw_feat[...] = home_feat[...]
        pair_load.wait()

    @pl.when(moves)
    def _():
        stage[...] = unit
        pl.semaphore_wait(go, 1)
        for which in swap_order:
            swap_unit(which, x).start()
        swap_pair.start()
        for order in range(CHUNKS // 2):
            for which in (order, CHUNKS - 1 - order):
                swap_unit(which, core).wait_recv()
            for way in range(2):
                ring_copy(way, 0, order).start()
            for which in (order, CHUNKS - 1 - order):
                sib_copy(z, which).start()
        for order in range(CHUNKS // 2, CHUNKS):
            for way in range(2):
                ring_copy(way, 0, order).start()
        swap_pair.wait_recv()

    unit_t[...] = u_all[z, pl.ds(pl.multiple_of(core * ROWS, ROWS), ROWS), :].T
    totals[...] = jnp.zeros_like(totals)
    pull_one[...] = jnp.zeros_like(pull_one)
    pull_pos[...] = jnp.zeros_like(pull_pos)

    def column_ids(zz):
        return lax.broadcasted_iota(jnp.int32, (PAIR, ROWS), 0) + zz * PAIR

    def block_of(step):
        hop = (step + 1) // 2
        return ring(jnp.where(lax.rem(step, 2) == 1, -hop, hop))

    def score_part(zz):
        score = dot(u_all[zz], unit_t[...])
        own = lax.broadcasted_iota(jnp.int32, (1, ROWS), 1) + (z * PAIR + core * ROWS)
        expo = jnp.where(column_ids(zz) != own, jnp.exp2(score * exp2_scale - exp2_scale), 0.0)
        totals[...] += jnp.sum(expo, 0, keepdims=True)
        expo_all[zz] = expo.astype(jnp.bfloat16)

    def pull_part(zz):
        ut_all[zz] = u_all[zz].T
        columns[:, :ROWS] = expo_all[zz]
        columns[:, ROWS:] = jnp.where(column_ids(zz) == partner[...], 1.0, 0.0).astype(jnp.bfloat16)
        both = dot(ut_all[zz], columns[...])
        pull_one[...] += both[:, :ROWS]
        pull_pos[...] += both[:, ROWS:]

    def send_on(way, hop, order):
        @pl.when(hop <= (3 if order < CHUNKS // 2 else 2))
        def _():
            ring_copy(way, hop, order).start()

        source = ring(-hop) if way == 0 else ring(hop)
        sib_copy(source, order_chunk(way, order)).start()

    def pass_on(hop, order):
        for way in range(2):
            source = ring(-hop) if way == 0 else ring(hop)
            ref = chunk_of(source, core, order_chunk(way, order))
            index = CHUNKS * (hop - 1) + order
            remote(ref, ref, ring_s.at[way, index], ring_r.at[way, index], sibling).wait_recv()
            send_on(way, hop, order)

    def events(k, part):
        hop = k // 2 + 1
        group = CHUNKS // 4
        for odd in range(2):
            orders = [odd * (CHUNKS // 2) + part * group + i for i in range(group)]

            @pl.when(lax.rem(k, 2) == odd)
            def _():
                for order in orders:
                    pass_on(hop, order)

    def gather_step(step, carry):
        group = jnp.minimum(step, 6)

        @pl.when(step != 6)
        def _():
            events(group, 0)

        @pl.when(step > 0)
        def _():
            pull_part(block_of(step - 1))

        @pl.when(step != 6)
        def _():
            events(group, 1)

        @pl.when((step == 3) & moves)
        def _():
            for copy in swap_raw():
                copy.start()

        @pl.when(step == 6)
        def _():
            @pl.when(moves)
            def _():
                for copy in swap_raw():
                    copy.wait_recv()

            summed_t[...] = (raw_clip[...].astype(jnp.float32) + raw_feat[...].astype(jnp.float32)).T

        zz = block_of(step)
        for which in range(CHUNKS):
            sib_arrival(zz, which).wait_recv()
        score_part(zz)
        return carry

    lax.fori_loop(0, ZS, gather_step, 0)

    tot_all[z, core] = totals[...]
    others = [(dz, dc) for dz in (4, 3, 5, 2, 6, 1, 7, 0) for dc in range(2) if dz or dc]

    def total_copy(dz, dc):
        ref = tot_all.at[z, core]
        return remote(ref, ref, tot_s.at[dz, dc], tot_r.at[z, core], at(ring(dz), x, peer, lax.rem(core + dc, 2)))

    def total_arrival(zz, block):
        ref = tot_all.at[zz, block]
        return remote(ref, ref, tot_s.at[0, 0], tot_r.at[zz, block], sibling)

    loss_copy = remote(loss_stage, loss_ret, ret_s.at[PARTS], ret_r.at[PARTS], swapped)

    for dz, dc in others:
        total_copy(dz, dc).start()
    pull_part(block_of(ZS - 1))

    @pl.when(moves)
    def _():
        pl.semaphore_wait(barrier, PEERS)
        greet(at(z, 1 - x, peer, core), peers_in)


    inverse = 1.0 / totals[...]
    positive = jnp.sum(unit_t[...].astype(jnp.float32) * pull_pos[...], 0, keepdims=True)
    loss = logit_scale * (1.0 - positive) + jnp.log(totals[...])

    @pl.when(stays)
    def _():
        loss_out[...] = loss

    @pl.when(moves)
    def _():
        loss_stage[...] = loss
        loss_copy.start()
    acc[...] = inverse * pull_one[...] - 2.0 * pull_pos[...]
    factor_t = lax.rsqrt(jnp.sum(summed_t[...] * summed_t[...], 0, keepdims=True) + E * norm_eps)

    def second(zz, own):
        if not own:
            total_arrival(zz, core).wait_recv()
        total_arrival(zz, 1 - core).wait_recv()
        scale = 1.0 / jnp.concatenate([tot_all[zz, 0], tot_all[zz, 1]], 1)
        scaled = (ut_all[zz].astype(jnp.float32) * scale).astype(jnp.bfloat16)
        return dot(scaled, expo_all[zz])

    def second_hop(hop, carry):
        acc[...] += second(ring(-hop), False) + second(ring(hop), False)
        return carry

    acc[...] += second(z, True)
    lax.fori_loop(1, 4, second_hop, 0)
    last = ring(4)
    total_arrival(last, core).wait_recv()
    total_arrival(last, 1 - core).wait_recv()
    scale = 1.0 / jnp.concatenate([tot_all[last, 0], tot_all[last, 1]], 1)
    scaled_last[...] = (ut_all[last].astype(jnp.float32) * scale).astype(jnp.bfloat16)

    def part_rows(part):
        return slice(part * PART, (part + 1) * PART)

    def ret_copy(part):
        rows = pl.ds(part * PART, PART)
        return remote(ret_stage.at[rows], ret.at[rows], ret_s.at[part], ret_r.at[part], swapped)

    def piece_rows(part, owner):
        return pl.ds(pl.multiple_of(part * PART + owner * PIECE, PIECE), PIECE)

    def rs_copy(part, d, crosses):
        owner = lax.rem(peer + d, PEERS)
        source = peer + PEERS if crosses else peer
        return remote(ret_stage.at[piece_rows(part, owner)], rs_buf.at[part, source], rs_s.at[part, d], rs_r.at[part, source],
                      at(z, 1 - x if crosses else x, owner, core))

    def rs_arrival(part, source):
        ref = rs_buf.at[part, source]
        return remote(ref, ref, rs_s.at[part, 0], rs_r.at[part, source], sibling)

    far_first = (4, 3, 5, 2, 6, 1, 7)

    @pl.when(stays)
    def _():
        pl.semaphore_wait(peers_in, 1)

    for part in range(PARTS):
        rows = part_rows(part)
        field = acc[:, rows]
        field += dot(scaled_last[...], expo_all[ring(4), :, rows])
        grad_unit = logit_scale * field
        summed_part = summed_t[:, rows]
        factor_part = factor_t[:, rows]
        along = jnp.sum(summed_part * grad_unit, 0, keepdims=True)
        grad = (factor_part * grad_unit - factor_part**3 * along * summed_part).T

        @pl.when(stays)
        def _():
            ret_stage[rows, :] = grad.astype(jnp.bfloat16)
            for d in far_first:
                rs_copy(part, d, False).start()
            seg_out[0, rows, :] = grad
            rs_buf[part, peer] = ret_stage[piece_rows(part, peer), :]

        @pl.when(moves)
        def _():
            ret_stage[rows, :] = grad.astype(jnp.bfloat16)
            for d in far_first + (0,):
                rs_copy(part, d, True).start()

    @pl.when(moves)
    def _():
        for part in range(PARTS):
            ret_copy(part).start()

    for way in range(2):
        for index in range(RING_COPIES):
            ring_copy(way, index // CHUNKS, index % CHUNKS).wait_send()
    for zz in range(ZS):
        for which in range(CHUNKS):
            sib_copy(zz, which).wait_send()
    for dz, dc in others:
        total_copy(dz, dc).wait_send()

    @pl.when(moves)
    def _():
        for which in range(CHUNKS):
            swap_unit(which, x).wait_send()
        swap_pair.wait_send()
        for copy in swap_raw():
            copy.wait_send()
        loss_copy.wait_send()

    def gathered_rows(part, owner):
        return gathered.at[pl.ds(pl.multiple_of(part * PART + owner * PIECE, PIECE), PIECE)]

    def ag_copy(part, d):
        ref = gathered_rows(part, peer)
        return remote(ref, ref, ag_s.at[part, d], ag_r.at[part, peer], at(z, x, lax.rem(peer + d, PEERS), core))

    def ag_arrival(part, source):
        ref = gathered_rows(part, source)
        return remote(ref, ref, ag_s.at[part, 0], ag_r.at[part, source], sibling)

    def fin_copy(part):
        ref = gathered.at[pl.ds(part * PART, PART)]
        return remote(ref, ref, fin_s.at[part], fin_r.at[part], sibling)

    @pl.when(stays)
    def _():
        for part in range(PARTS):
            for d in far_first[::-1]:
                rs_arrival(part, lax.rem(peer + d, PEERS)).wait_recv()
            for d in range(PEERS):
                rs_arrival(part, PEERS + lax.rem(peer + d, PEERS)).wait_recv()
            reduced = rs_buf[part, 0].astype(jnp.float32)
            for source in range(1, 2 * PEERS):
                reduced += rs_buf[part, source].astype(jnp.float32)
            gathered[piece_rows(part, peer), :] = reduced.astype(jnp.bfloat16)
            for d in far_first:
                ag_copy(part, d).start()
        for part in range(PARTS):
            for d in far_first:
                rs_copy(part, d, False).wait_send()
        for part in range(PARTS):
            for d in far_first[::-1]:
                ag_arrival(part, lax.rem(peer + PEERS - d, PEERS)).wait_recv()
            fin_copy(part).start()
        for part in range(PARTS):
            for d in far_first:
                ag_copy(part, d).wait_send()
            fin_copy(part).wait_send()

    @pl.when(moves)
    def _():
        loss_copy.wait_recv()
        loss_out[...] = loss_ret[...]
        for part in range(PARTS):
            rows = part_rows(part)
            ret_copy(part).wait_recv()
            seg_out[0, rows, :] = ret[rows, :].astype(jnp.float32)
        for part in range(PARTS):
            ret_copy(part).wait_send()
            for d in range(PEERS):
                rs_copy(part, d, True).wait_send()
        for part in range(PARTS):
            fin_copy(part).wait_recv()


def hand_over(loss_in, seg_in, sum_in, loss_out, seg_out, clip_out, wide, sems):
    copies = [
        pltpu.make_async_copy(seg_in, seg_out, sems.at[0]),
        pltpu.make_async_copy(loss_in, loss_out, sems.at[1]),
        pltpu.make_async_copy(wide, clip_out, sems.at[2]),
    ]
    for copy in copies[:2]:
        copy.start()
    wide[...] = sum_in[...].astype(jnp.float32)
    copies[2].start()
    for copy in copies:
        copy.wait()


def on_device(clip_embed, seg_feats, pair_index):
    bf16, f32, i32 = jnp.bfloat16, jnp.float32, jnp.int32
    vmem = pl.BlockSpec(memory_space=pltpu.VMEM)
    anywhere = pl.BlockSpec(memory_space=pl.ANY)
    hbm = pl.BlockSpec(memory_space=pltpu.HBM)
    dma = pltpu.SemaphoreType.DMA
    loss, seg, total = pl.pallas_call(
        kernel,
        name="ntxent",
        out_shape=(
            pltpu.VMEM((1, ROWS), f32),
            pltpu.VMEM((1, ROWS, E), f32),
            pltpu.VMEM((ROWS, E), bf16),
        ),
        in_specs=[hbm] * 3,
        out_specs=(vmem,) * 3,
        scratch_shapes=[
            pltpu.VMEM((ZS, PAIR, E), bf16),
            pltpu.VMEM((ZS, E, PAIR), bf16),
            pltpu.VMEM((ZS, PAIR, ROWS), bf16),
            pltpu.VMEM((PAIR, 2 * ROWS), bf16),
            pltpu.VMEM((E, PAIR), bf16),
            pltpu.VMEM((ZS, 2, 1, ROWS), f32),
            pltpu.VMEM((E, ROWS), bf16),
            pltpu.VMEM((ROWS, E), bf16),
            pltpu.VMEM((ROWS, E), bf16),
            pltpu.VMEM((ROWS, E), bf16),
            pltpu.VMEM((ROWS, E), bf16),
            pltpu.VMEM((ROWS, E), bf16),
            pltpu.VMEM((1, ROWS), i32),
            pltpu.VMEM((1, ROWS), f32),
            pltpu.VMEM((E, ROWS), f32),
            pltpu.VMEM((E, ROWS), f32),
            pltpu.VMEM((E, ROWS), f32),
            pltpu.VMEM((E, ROWS), f32),
            pltpu.VMEM((ROWS, E), bf16),
            pltpu.VMEM((ROWS, E), bf16),
            pltpu.VMEM((1, ROWS), f32),
            pltpu.VMEM((1, ROWS), f32),
            pltpu.VMEM((PARTS, 2 * PEERS, PIECE, E), bf16),
            dma((3,)),
            dma((CHUNKS + 3,)), dma((CHUNKS + 3,)),
            dma((2, RING_COPIES)), dma((2, RING_COPIES)),
            dma((ZS, CHUNKS)), dma((ZS, CHUNKS)),
            dma((ZS, 2)), dma((ZS, 2)),
            dma((PARTS + 1,)), dma((PARTS + 1,)),
            dma((PARTS, PEERS)), dma((PARTS, 2 * PEERS)),
            dma((PARTS, PEERS)), dma((PARTS, PEERS)),
            dma((PARTS,)), dma((PARTS,)),
            pltpu.SemaphoreType.REGULAR, pltpu.SemaphoreType.REGULAR, pltpu.SemaphoreType.REGULAR,
        ],
        compiler_params=pltpu.CompilerParams(
            collective_id=0, has_side_effects=True, vmem_limit_bytes=56 * 2**20
        ),
    )(clip_embed, seg_feats, pair_index)
    return pl.pallas_call(
        hand_over,
        name="hand_over",
        out_shape=(
            jax.ShapeDtypeStruct((1, ROWS), f32),
            jax.ShapeDtypeStruct((1, ROWS, E), f32),
            jax.ShapeDtypeStruct((ROWS, E), f32),
        ),
        in_specs=[vmem] * 3,
        out_specs=(anywhere,) * 3,
        scratch_shapes=[pltpu.VMEM((ROWS, E), f32), dma((3,))],
        compiler_params=pltpu.CompilerParams(vmem_limit_bytes=4 * 2**20),
    )(loss, seg, total)


def solution(mesh):
    placed = (P("clip", None), P("tm", "clip", None), P("tm", "clip"))
    return jax.shard_map(
        on_device,
        mesh=mesh,
        in_specs=placed,
        out_specs=(P("tm", "clip"), P("tm", "clip", None), P("clip", None)),
        check_vma=False,
    )
```

```python
import math

import jax
import jax.numpy as jnp
from jax import lax
from jax.experimental import pallas as pl
from jax.experimental.pallas import tpu as pltpu
from jax.sharding import PartitionSpec as P

MESH = pl.DeviceIdType.MESH
logit_scale = 14.0
norm_eps = 1e-06
exp2_scale = logit_scale * math.log2(math.e)

ZS = 8
ROWS = 384
CHUNKS = 4
CHUNK = ROWS // CHUNKS
PAIR = 2 * ROWS
E = 512
PEERS = 8
PARTS = 3
PART = ROWS // PARTS
PIECE = PART // PEERS
RING_COPIES = CHUNKS * 7 // 2


def remote(src, dst, send_sem, recv_sem, device):
    return pltpu.make_async_remote_copy(
        src_ref=src, dst_ref=dst, send_sem=send_sem, recv_sem=recv_sem,
        device_id=device, device_id_type=MESH,
    )


def dot(a, b):
    return jnp.dot(a, b, preferred_element_type=jnp.float32)


def kernel(
    clip_hbm, feat_hbm, pair_hbm,
    loss_out, seg_out, gathered,
    u_all, ut_all, expo_all, columns, scaled_last, tot_all, unit_t, stage, raw_clip, raw_feat, home_clip, home_feat, partner, totals,
    pull_one, pull_pos, acc, summed_t, ret_stage, ret, loss_stage, loss_ret,
    rs_buf,
    load_s, swap_s, swap_r, ring_s, ring_r, sib_s, sib_r, tot_s, tot_r, ret_s, ret_r,
    rs_s, rs_r, ag_s, ag_r, last_s, last_r, fin_s, fin_r, near, go, peers_in,
):
    clip = lax.axis_index("clip")
    tm = lax.axis_index("tm")
    z, x = clip // 2, lax.rem(clip, 2)
    peer, core = tm // 2, lax.rem(tm, 2)
    stays = x == core
    moves = x != core

    def at(zz, xx, pp, cc):
        return (zz * 2 + xx, pp * 2 + cc)

    def ring(offset):
        return lax.rem(z + offset + ZS, ZS)

    sibling = at(z, x, peer, 1 - core)
    swapped = at(z, 1 - x, peer, 1 - core)

    barrier = pltpu.get_barrier_semaphore()

    def greet(device, semaphore):
        pl.semaphore_signal(semaphore, inc=1, device_id=device, device_id_type=MESH)

    neighbours = [at(ring(1), x, peer, core), at(ring(-1), x, peer, core), swapped]

    @pl.when(stays)
    def _():
        for device in neighbours:
            greet(device, barrier)
        for d in range(PEERS):
            greet(at(z, 1 - x, lax.rem(peer + d, PEERS), core), barrier)

    @pl.when(moves)
    def _():
        greet(sibling, barrier)

    chunk_order = [c for o in range(CHUNKS // 2) for c in (o, CHUNKS - 1 - o)]
    pair_load = pltpu.make_async_copy(pair_hbm, partner, load_s.at[2, 0])

    def chunk_loads(which):
        rows = pl.ds(which * CHUNK, CHUNK)
        return [
            pltpu.make_async_copy(clip_hbm.at[rows], home_clip.at[rows], load_s.at[0, which]),
            pltpu.make_async_copy(feat_hbm.at[0, rows], home_feat.at[rows], load_s.at[1, which]),
        ]

    for which in chunk_order:
        for load in chunk_loads(which):
            load.start()

    def unit_chunk(which):
        rows = slice(which * CHUNK, (which + 1) * CHUNK)
        for load in chunk_loads(which):
            load.wait()
        summed = home_clip[rows, :].astype(jnp.float32) + home_feat[rows, :].astype(jnp.float32)
        factor = lax.rsqrt(jnp.sum(summed * summed, 1, keepdims=True) + E * norm_eps)
        return (summed * factor).astype(jnp.bfloat16)

    def chunk_of(zz, block, which):
        return u_all.at[zz, pl.ds(pl.multiple_of(block * ROWS + which * CHUNK, CHUNK), CHUNK)]

    def swap_unit(which, block):
        return remote(stage.at[pl.ds(which * CHUNK, CHUNK)], chunk_of(z, block, which),
                      swap_s.at[which], swap_r.at[which], swapped)

    def swap_raw():
        return [
            remote(feat_hbm.at[0], raw_feat, swap_s.at[CHUNKS], swap_r.at[CHUNKS], swapped),
            remote(clip_hbm, raw_clip, swap_s.at[CHUNKS + 1], swap_r.at[CHUNKS + 1], swapped),
        ]

    swap_pair = remote(pair_hbm, partner, swap_s.at[CHUNKS + 2], swap_r.at[CHUNKS + 2], swapped)

    def order_chunk(way, order):
        return order if way == 0 else CHUNKS - 1 - order

    def ring_copy(way, hop, order):
        source, target = (ring(-hop), ring(1)) if way == 0 else (ring(hop), ring(-1))
        ref = chunk_of(source, core, order_chunk(way, order))
        index = CHUNKS * hop + order
        return remote(ref, ref, ring_s.at[way, index], ring_r.at[way, index], at(target, x, peer, core))

    def sib_copy(source, which):
        ref = chunk_of(source, core, which)
        return remote(ref, ref, sib_s.at[source, which], sib_r.at[source, which], sibling)

    def sib_arrival(source, which):
        ref = chunk_of(source, 1 - core, which)
        return remote(ref, ref, sib_s.at[source, which], sib_r.at[source, which], sibling)


    @pl.when(stays)
    def _():
        pair_load.start()
        pl.semaphore_wait(barrier, 4)
        for device in neighbours:
            greet(device, near)
        for order in range(CHUNKS // 2):
            for way in range(2):
                which = order_chunk(way, order)
                rows = pl.ds(pl.multiple_of(core * ROWS + which * CHUNK, CHUNK), CHUNK)
                u_all[z, rows, :] = unit_chunk(which)
                ring_copy(way, 0, order).start()
            if order == 0:
                pl.semaphore_wait(near, 3)
                greet(sibling, go)
        for order in range(CHUNKS // 2, CHUNKS):
            for way in range(2):
                ring_copy(way, 0, order).start()
        for which in chunk_order:
            sib_copy(z, which).start()
        raw_clip[...] = home_clip[...]
        raw_feat[...] = home_feat[...]
        pair_load.wait()

    @pl.when(moves)
    def _():
        for which in chunk_order:
            stage[which * CHUNK:(which + 1) * CHUNK, :] = unit_chunk(which)
        pl.semaphore_wait(go, 1)
        for which in chunk_order:
            swap_unit(which, x).start()
        swap_pair.start()
        for order in range(CHUNKS // 2):
            for which in (order, CHUNKS - 1 - order):
                swap_unit(which, core).wait_recv()
            for way in range(2):
                ring_copy(way, 0, order).start()
            for which in (order, CHUNKS - 1 - order):
                sib_copy(z, which).start()
        for order in range(CHUNKS // 2, CHUNKS):
            for way in range(2):
                ring_copy(way, 0, order).start()
        swap_pair.wait_recv()

    unit_t[...] = u_all[z, pl.ds(pl.multiple_of(core * ROWS, ROWS), ROWS), :].T
    totals[...] = jnp.zeros_like(totals)
    pull_one[...] = jnp.zeros_like(pull_one)
    pull_pos[...] = jnp.zeros_like(pull_pos)

    def column_ids(zz):
        return lax.broadcasted_iota(jnp.int32, (PAIR, ROWS), 0) + zz * PAIR

    def block_of(step):
        hop = (step + 1) // 2
        return ring(jnp.where(lax.rem(step, 2) == 1, -hop, hop))

    def score_part(zz, block):
        rows = pl.ds(pl.multiple_of(block * ROWS, ROWS), ROWS)
        score = dot(u_all[zz, rows, :], unit_t[...])
        ids = lax.broadcasted_iota(jnp.int32, (ROWS, ROWS), 0) + (zz * PAIR + block * ROWS)
        own = lax.broadcasted_iota(jnp.int32, (1, ROWS), 1) + (z * PAIR + core * ROWS)
        expo = jnp.where(ids != own, jnp.exp2(score * exp2_scale - exp2_scale), 0.0)
        totals[...] += jnp.sum(expo, 0, keepdims=True)
        expo_all[zz, rows, :] = expo.astype(jnp.bfloat16)

    def pull_part(zz):
        ut_all[zz] = u_all[zz].T
        columns[:, :ROWS] = expo_all[zz]
        columns[:, ROWS:] = jnp.where(column_ids(zz) == partner[...], 1.0, 0.0).astype(jnp.bfloat16)
        both = dot(ut_all[zz], columns[...])
        pull_one[...] += both[:, :ROWS]
        pull_pos[...] += both[:, ROWS:]

    def send_on(way, hop, order):
        @pl.when(hop <= (3 if order < CHUNKS // 2 else 2))
        def _():
            ring_copy(way, hop, order).start()

        source = ring(-hop) if way == 0 else ring(hop)
        sib_copy(source, order_chunk(way, order)).start()

    def pass_on(hop, order):
        for way in range(2):
            source = ring(-hop) if way == 0 else ring(hop)
            ref = chunk_of(source, core, order_chunk(way, order))
            index = CHUNKS * (hop - 1) + order
            remote(ref, ref, ring_s.at[way, index], ring_r.at[way, index], sibling).wait_recv()
            send_on(way, hop, order)

    def events(k, part):
        hop = k // 2 + 1
        group = CHUNKS // 4
        for odd in range(2):
            orders = [odd * (CHUNKS // 2) + part * group + i for i in range(group)]

            @pl.when(lax.rem(k, 2) == odd)
            def _():
                for order in orders:
                    pass_on(hop, order)

    def gather_step(step, carry):
        group = jnp.minimum(step, 6)

        @pl.when(step != 6)
        def _():
            events(group, 0)

        @pl.when(step > 0)
        def _():
            pull_part(block_of(step - 1))

        @pl.when(step != 6)
        def _():
            events(group, 1)

        @pl.when((step == 3) & moves)
        def _():
            for copy in swap_raw():
                copy.start()

        @pl.when(step == 6)
        def _():
            @pl.when(moves)
            def _():
                for copy in swap_raw():
                    copy.wait_recv()

            summed_t[...] = (raw_clip[...].astype(jnp.float32) + raw_feat[...].astype(jnp.float32)).T

        zz = block_of(step)
        score_part(zz, core)
        for which in range(CHUNKS):
            sib_arrival(zz, which).wait_recv()
        score_part(zz, 1 - core)
        return carry

    lax.fori_loop(0, ZS, gather_step, 0)

    tot_all[z, core] = totals[...]
    others = [(dz, dc) for dz in (4, 3, 5, 2, 6, 1, 7, 0) for dc in range(2) if dz or dc]

    def total_copy(dz, dc):
        ref = tot_all.at[z, core]
        return remote(ref, ref, tot_s.at[dz, dc], tot_r.at[z, core], at(ring(dz), x, peer, lax.rem(core + dc, 2)))

    def total_arrival(zz, block):
        ref = tot_all.at[zz, block]
        return remote(ref, ref, tot_s.at[0, 0], tot_r.at[zz, block], sibling)

    loss_copy = remote(loss_stage, loss_ret, ret_s.at[PARTS], ret_r.at[PARTS], swapped)

    for dz, dc in others:
        total_copy(dz, dc).start()
    pull_part(block_of(ZS - 1))

    @pl.when(moves)
    def _():
        pl.semaphore_wait(barrier, PEERS)
        greet(at(z, 1 - x, peer, core), peers_in)


    inverse = 1.0 / totals[...]
    positive = jnp.sum(unit_t[...].astype(jnp.float32) * pull_pos[...], 0, keepdims=True)
    loss = logit_scale * (1.0 - positive) + jnp.log(totals[...])

    @pl.when(stays)
    def _():
        loss_out[...] = loss

    @pl.when(moves)
    def _():
        loss_stage[...] = loss
        loss_copy.start()
    acc[...] = inverse * pull_one[...] - 2.0 * pull_pos[...]
    factor_t = lax.rsqrt(jnp.sum(summed_t[...] * summed_t[...], 0, keepdims=True) + E * norm_eps)

    def second(zz, own):
        if not own:
            total_arrival(zz, core).wait_recv()
        total_arrival(zz, 1 - core).wait_recv()
        scale = 1.0 / jnp.concatenate([tot_all[zz, 0], tot_all[zz, 1]], 1)
        scaled = (ut_all[zz].astype(jnp.float32) * scale).astype(jnp.bfloat16)
        return dot(scaled, expo_all[zz])

    def second_hop(hop, carry):
        acc[...] += second(ring(-hop), False) + second(ring(hop), False)
        return carry

    acc[...] += second(z, True)
    for hop in range(1, 4):
        second_hop(hop, 0)
    last = ring(4)
    total_arrival(last, core).wait_recv()
    total_arrival(last, 1 - core).wait_recv()
    scale = 1.0 / jnp.concatenate([tot_all[last, 0], tot_all[last, 1]], 1)
    scaled = (ut_all[last].astype(jnp.float32) * scale).astype(jnp.bfloat16)
    scaled_last[...] = scaled

    def part_rows(part):
        return slice(part * PART, (part + 1) * PART)

    def ret_copy(part):
        rows = pl.ds(part * PART, PART)
        return remote(ret_stage.at[rows], ret.at[rows], ret_s.at[part], ret_r.at[part], swapped)

    def piece_rows(part, owner):
        return pl.ds(pl.multiple_of(part * PART + owner * PIECE, PIECE), PIECE)

    def rs_copy(part, d, crosses):
        owner = lax.rem(peer + d, PEERS)
        source = peer + PEERS if crosses else peer
        return remote(ret_stage.at[piece_rows(part, owner)], rs_buf.at[part, source], rs_s.at[part, d], rs_r.at[part, source],
                      at(z, 1 - x if crosses else x, owner, core))

    def rs_arrival(part, source):
        ref = rs_buf.at[part, source]
        return remote(ref, ref, rs_s.at[part, 0], rs_r.at[part, source], sibling)

    far_first = (4, 3, 5, 2, 6, 1, 7)

    @pl.when(stays)
    def _():
        pl.semaphore_wait(peers_in, 1)

    for part in range(PARTS):
        rows = part_rows(part)
        field = acc[:, rows]
        field += dot(scaled_last[...], expo_all[ring(4), :, rows])
        grad_unit = logit_scale * field
        summed_part = summed_t[:, rows]
        factor_part = factor_t[:, rows]
        along = jnp.sum(summed_part * grad_unit, 0, keepdims=True)
        grad = (factor_part * grad_unit - factor_part**3 * along * summed_part).T

        @pl.when(stays)
        def _():
            ret_stage[rows, :] = grad.astype(jnp.bfloat16)
            for d in far_first:
                rs_copy(part, d, False).start()
            seg_out[0, rows, :] = grad
            rs_buf[part, peer] = ret_stage[piece_rows(part, peer), :]

        @pl.when(moves)
        def _():
            ret_stage[rows, :] = grad.astype(jnp.bfloat16)
            for d in far_first + (0,):
                rs_copy(part, d, True).start()

    @pl.when(moves)
    def _():
        for part in range(PARTS):
            ret_copy(part).start()

    for way in range(2):
        for index in range(RING_COPIES):
            ring_copy(way, index // CHUNKS, index % CHUNKS).wait_send()
    for zz in range(ZS):
        for which in range(CHUNKS):
            sib_copy(zz, which).wait_send()
    for dz, dc in others:
        total_copy(dz, dc).wait_send()

    @pl.when(moves)
    def _():
        for which in range(CHUNKS):
            swap_unit(which, x).wait_send()
        swap_pair.wait_send()
        for copy in swap_raw():
            copy.wait_send()
        loss_copy.wait_send()

    def gathered_rows(part, owner):
        return gathered.at[pl.ds(pl.multiple_of(part * PART + owner * PIECE, PIECE), PIECE)]

    def ag_copy(part, d):
        ref = gathered_rows(part, peer)
        return remote(ref, ref, ag_s.at[part, d], ag_r.at[part, peer], at(z, x, lax.rem(peer + d, PEERS), core))

    def ag_arrival(part, source):
        ref = gathered_rows(part, source)
        return remote(ref, ref, ag_s.at[part, 0], ag_r.at[part, source], sibling)

    def last_copy(d):
        ref = gathered_rows(PARTS - 1, peer)
        return remote(ref, ref, last_s.at[d], last_r.at[peer], at(z, x, lax.rem(peer + d, PEERS), 1 - core))

    def last_arrival(source):
        ref = gathered_rows(PARTS - 1, source)
        return remote(ref, ref, last_s.at[0], last_r.at[source], sibling)

    def fin_copy(part):
        ref = gathered.at[pl.ds(part * PART, PART)]
        return remote(ref, ref, fin_s.at[part], fin_r.at[part], sibling)

    @pl.when(stays)
    def _():
        for part in range(PARTS):
            for d in far_first[::-1]:
                rs_arrival(part, lax.rem(peer + d, PEERS)).wait_recv()
            for d in range(PEERS):
                rs_arrival(part, PEERS + lax.rem(peer + d, PEERS)).wait_recv()
            reduced = rs_buf[part, 0].astype(jnp.float32)
            for source in range(1, 2 * PEERS):
                reduced += rs_buf[part, source].astype(jnp.float32)
            gathered[piece_rows(part, peer), :] = reduced.astype(jnp.bfloat16)
            for d in far_first:
                ag_copy(part, d).start()
                if part == PARTS - 1:
                    last_copy(d).start()
            if part == PARTS - 1:
                last_copy(0).start()
        for part in range(PARTS):
            for d in far_first:
                rs_copy(part, d, False).wait_send()
        for part in range(PARTS):
            for d in far_first[::-1]:
                ag_arrival(part, lax.rem(peer + PEERS - d, PEERS)).wait_recv()
            if part < PARTS - 1:
                fin_copy(part).start()
        for part in range(PARTS):
            for d in far_first:
                ag_copy(part, d).wait_send()
            if part < PARTS - 1:
                fin_copy(part).wait_send()
        for d in range(PEERS):
            last_copy(d).wait_send()

    @pl.when(moves)
    def _():
        loss_copy.wait_recv()
        loss_out[...] = loss_ret[...]
        for part in range(PARTS):
            rows = part_rows(part)
            ret_copy(part).wait_recv()
            seg_out[0, rows, :] = ret[rows, :].astype(jnp.float32)
        for part in range(PARTS):
            ret_copy(part).wait_send()
            for d in range(PEERS):
                rs_copy(part, d, True).wait_send()
        for part in range(PARTS):
            if part < PARTS - 1:
                fin_copy(part).wait_recv()
        for d in (0,) + far_first[::-1]:
            last_arrival(lax.rem(peer + PEERS - d, PEERS)).wait_recv()


def hand_over(loss_in, seg_in, sum_in, loss_out, seg_out, clip_out, wide, sems):
    copies = [
        pltpu.make_async_copy(seg_in, seg_out, sems.at[0]),
        pltpu.make_async_copy(loss_in, loss_out, sems.at[1]),
        pltpu.make_async_copy(wide, clip_out, sems.at[2]),
    ]
    for copy in copies[:2]:
        copy.start()
    wide[...] = sum_in[...].astype(jnp.float32)
    copies[2].start()
    for copy in copies:
        copy.wait()


def on_device(clip_embed, seg_feats, pair_index):
    bf16, f32, i32 = jnp.bfloat16, jnp.float32, jnp.int32
    vmem = pl.BlockSpec(memory_space=pltpu.VMEM)
    anywhere = pl.BlockSpec(memory_space=pl.ANY)
    hbm = pl.BlockSpec(memory_space=pltpu.HBM)
    dma = pltpu.SemaphoreType.DMA
    loss, seg, total = pl.pallas_call(
        kernel,
        name="ntxent",
        out_shape=(
            pltpu.VMEM((1, ROWS), f32),
            pltpu.VMEM((1, ROWS, E), f32),
            pltpu.VMEM((ROWS, E), bf16),
        ),
        in_specs=[hbm] * 3,
        out_specs=(vmem,) * 3,
        scratch_shapes=[
            pltpu.VMEM((ZS, PAIR, E), bf16),
            pltpu.VMEM((ZS, E, PAIR), bf16),
            pltpu.VMEM((ZS, PAIR, ROWS), bf16),
            pltpu.VMEM((PAIR, 2 * ROWS), bf16),
            pltpu.VMEM((E, PAIR), bf16),
            pltpu.VMEM((ZS, 2, 1, ROWS), f32),
            pltpu.VMEM((E, ROWS), bf16),
            pltpu.VMEM((ROWS, E), bf16),
            pltpu.VMEM((ROWS, E), bf16),
            pltpu.VMEM((ROWS, E), bf16),
            pltpu.VMEM((ROWS, E), bf16),
            pltpu.VMEM((ROWS, E), bf16),
            pltpu.VMEM((1, ROWS), i32),
            pltpu.VMEM((1, ROWS), f32),
            pltpu.VMEM((E, ROWS), f32),
            pltpu.VMEM((E, ROWS), f32),
            pltpu.VMEM((E, ROWS), f32),
            pltpu.VMEM((E, ROWS), f32),
            pltpu.VMEM((ROWS, E), bf16),
            pltpu.VMEM((ROWS, E), bf16),
            pltpu.VMEM((1, ROWS), f32),
            pltpu.VMEM((1, ROWS), f32),
            pltpu.VMEM((PARTS, 2 * PEERS, PIECE, E), bf16),
            dma((3, CHUNKS)),
            dma((CHUNKS + 3,)), dma((CHUNKS + 3,)),
            dma((2, RING_COPIES)), dma((2, RING_COPIES)),
            dma((ZS, CHUNKS)), dma((ZS, CHUNKS)),
            dma((ZS, 2)), dma((ZS, 2)),
            dma((PARTS + 1,)), dma((PARTS + 1,)),
            dma((PARTS, PEERS)), dma((PARTS, 2 * PEERS)),
            dma((PARTS, PEERS)), dma((PARTS, PEERS)),
            dma((PEERS,)), dma((PEERS,)),
            dma((PARTS,)), dma((PARTS,)),
            pltpu.SemaphoreType.REGULAR, pltpu.SemaphoreType.REGULAR, pltpu.SemaphoreType.REGULAR,
        ],
        compiler_params=pltpu.CompilerParams(
            collective_id=0, has_side_effects=True, vmem_limit_bytes=56 * 2**20
        ),
    )(clip_embed, seg_feats, pair_index)
    return pl.pallas_call(
        hand_over,
        name="hand_over",
        out_shape=(
            jax.ShapeDtypeStruct((1, ROWS), f32),
            jax.ShapeDtypeStruct((1, ROWS, E), f32),
            jax.ShapeDtypeStruct((ROWS, E), f32),
        ),
        in_specs=[vmem] * 3,
        out_specs=(anywhere,) * 3,
        scratch_shapes=[pltpu.VMEM((ROWS, E), f32), dma((3,))],
        compiler_params=pltpu.CompilerParams(vmem_limit_bytes=4 * 2**20),
    )(loss, seg, total)


def solution(mesh):
    placed = (P("clip", None), P("tm", "clip", None), P("tm", "clip"))
    return jax.shard_map(
        on_device,
        mesh=mesh,
        in_specs=placed,
        out_specs=(P("tm", "clip"), P("tm", "clip", None), P("clip", None)),
        check_vma=False,
    )
```

```python
import math

import jax
import jax.numpy as jnp
from jax import lax
from jax.experimental import pallas as pl
from jax.experimental.pallas import tpu as pltpu
from jax.sharding import PartitionSpec as P

MESH = pl.DeviceIdType.MESH
logit_scale = 14.0
norm_eps = 1e-06
exp2_scale = logit_scale * math.log2(math.e)

ZS = 8
ROWS = 384
CHUNKS = 4
CHUNK = ROWS // CHUNKS
PAIR = 2 * ROWS
E = 512
PEERS = 8
PARTS = 3
PART = ROWS // PARTS
PIECE = PART // PEERS
RING_COPIES = CHUNKS * 7 // 2


def remote(src, dst, send_sem, recv_sem, device):
    return pltpu.make_async_remote_copy(
        src_ref=src, dst_ref=dst, send_sem=send_sem, recv_sem=recv_sem,
        device_id=device, device_id_type=MESH,
    )


def dot(a, b):
    return jnp.dot(a, b, preferred_element_type=jnp.float32)


def kernel(
    clip_hbm, feat_hbm, pair_hbm,
    loss_out, seg_out, gathered,
    u_all, ut_all, expo_all, columns, scaled_last, tot_all, unit_t, stage, raw_clip, raw_feat, home_clip, home_feat, partner, totals,
    pull_one, pull_pos, acc, summed_t, ret_stage, ret, loss_stage, loss_ret,
    rs_buf,
    load_s, swap_s, swap_r, ring_s, ring_r, sib_s, sib_r, tot_s, tot_r, ret_s, ret_r,
    rs_s, rs_r, ag_s, ag_r, last_s, last_r, fin_s, fin_r, near, go, peers_in,
):
    clip = lax.axis_index("clip")
    tm = lax.axis_index("tm")
    z, x = clip // 2, lax.rem(clip, 2)
    peer, core = tm // 2, lax.rem(tm, 2)
    stays = x == core
    moves = x != core

    def at(zz, xx, pp, cc):
        return (zz * 2 + xx, pp * 2 + cc)

    def ring(offset):
        return lax.rem(z + offset + ZS, ZS)

    sibling = at(z, x, peer, 1 - core)
    swapped = at(z, 1 - x, peer, 1 - core)

    barrier = pltpu.get_barrier_semaphore()

    def greet(device, semaphore):
        pl.semaphore_signal(semaphore, inc=1, device_id=device, device_id_type=MESH)

    neighbours = [at(ring(1), x, peer, core), at(ring(-1), x, peer, core), swapped]

    @pl.when(stays)
    def _():
        for device in neighbours:
            greet(device, barrier)
        for d in range(PEERS):
            greet(at(z, 1 - x, lax.rem(peer + d, PEERS), core), barrier)

    @pl.when(moves)
    def _():
        greet(sibling, barrier)

    chunk_order = [c for o in range(CHUNKS // 2) for c in (o, CHUNKS - 1 - o)]
    pair_load = pltpu.make_async_copy(pair_hbm, partner, load_s.at[2, 0])

    def chunk_loads(which):
        rows = pl.ds(which * CHUNK, CHUNK)
        return [
            pltpu.make_async_copy(clip_hbm.at[rows], home_clip.at[rows], load_s.at[0, which]),
            pltpu.make_async_copy(feat_hbm.at[0, rows], home_feat.at[rows], load_s.at[1, which]),
        ]

    for which in chunk_order:
        for load in chunk_loads(which):
            load.start()

    def unit_chunk(which):
        rows = slice(which * CHUNK, (which + 1) * CHUNK)
        for load in chunk_loads(which):
            load.wait()
        summed = home_clip[rows, :].astype(jnp.float32) + home_feat[rows, :].astype(jnp.float32)
        factor = lax.rsqrt(jnp.sum(summed * summed, 1, keepdims=True) + E * norm_eps)
        return (summed * factor).astype(jnp.bfloat16)

    def chunk_of(zz, block, which):
        return u_all.at[zz, pl.ds(pl.multiple_of(block * ROWS + which * CHUNK, CHUNK), CHUNK)]

    def swap_unit(which, block):
        return remote(stage.at[pl.ds(which * CHUNK, CHUNK)], chunk_of(z, block, which),
                      swap_s.at[which], swap_r.at[which], swapped)

    def swap_raw():
        return [
            remote(feat_hbm.at[0], raw_feat, swap_s.at[CHUNKS], swap_r.at[CHUNKS], swapped),
            remote(clip_hbm, raw_clip, swap_s.at[CHUNKS + 1], swap_r.at[CHUNKS + 1], swapped),
        ]

    swap_pair = remote(pair_hbm, partner, swap_s.at[CHUNKS + 2], swap_r.at[CHUNKS + 2], swapped)

    def order_chunk(way, order):
        return order if way == 0 else CHUNKS - 1 - order

    def ring_copy(way, hop, order):
        source, target = (ring(-hop), ring(1)) if way == 0 else (ring(hop), ring(-1))
        ref = chunk_of(source, core, order_chunk(way, order))
        index = CHUNKS * hop + order
        return remote(ref, ref, ring_s.at[way, index], ring_r.at[way, index], at(target, x, peer, core))

    def sib_copy(source, which):
        ref = chunk_of(source, core, which)
        return remote(ref, ref, sib_s.at[source, which], sib_r.at[source, which], sibling)

    def sib_arrival(source, which):
        ref = chunk_of(source, 1 - core, which)
        return remote(ref, ref, sib_s.at[source, which], sib_r.at[source, which], sibling)


    @pl.when(stays)
    def _():
        pair_load.start()
        pl.semaphore_wait(barrier, 4)
        for device in neighbours:
            greet(device, near)
        for order in range(CHUNKS // 2):
            for way in range(2):
                which = order_chunk(way, order)
                rows = pl.ds(pl.multiple_of(core * ROWS + which * CHUNK, CHUNK), CHUNK)
                u_all[z, rows, :] = unit_chunk(which)
                ring_copy(way, 0, order).start()
            if order == 0:
                pl.semaphore_wait(near, 3)
                greet(sibling, go)
        for order in range(CHUNKS // 2, CHUNKS):
            for way in range(2):
                ring_copy(way, 0, order).start()
        for which in chunk_order:
            sib_copy(z, which).start()
        raw_clip[...] = home_clip[...]
        raw_feat[...] = home_feat[...]
        pair_load.wait()

    @pl.when(moves)
    def _():
        for which in chunk_order:
            stage[which * CHUNK:(which + 1) * CHUNK, :] = unit_chunk(which)
        pl.semaphore_wait(go, 1)
        for which in chunk_order:
            swap_unit(which, x).start()
        swap_pair.start()
        for order in range(CHUNKS // 2):
            for which in (order, CHUNKS - 1 - order):
                swap_unit(which, core).wait_recv()
            for way in range(2):
                ring_copy(way, 0, order).start()
            for which in (order, CHUNKS - 1 - order):
                sib_copy(z, which).start()
        for order in range(CHUNKS // 2, CHUNKS):
            for way in range(2):
                ring_copy(way, 0, order).start()
        swap_pair.wait_recv()

    unit_t[...] = u_all[z, pl.ds(pl.multiple_of(core * ROWS, ROWS), ROWS), :].T
    totals[...] = jnp.zeros_like(totals)
    pull_one[...] = jnp.zeros_like(pull_one)
    pull_pos[...] = jnp.zeros_like(pull_pos)

    def column_ids(zz):
        return lax.broadcasted_iota(jnp.int32, (PAIR, ROWS), 0) + zz * PAIR

    def block_of(step):
        hop = (step + 1) // 2
        return ring(jnp.where(lax.rem(step, 2) == 1, -hop, hop))

    def score_part(zz, block):
        rows = pl.ds(pl.multiple_of(block * ROWS, ROWS), ROWS)
        score = dot(u_all[zz, rows, :], unit_t[...])
        ids = lax.broadcasted_iota(jnp.int32, (ROWS, ROWS), 0) + (zz * PAIR + block * ROWS)
        own = lax.broadcasted_iota(jnp.int32, (1, ROWS), 1) + (z * PAIR + core * ROWS)
        expo = jnp.where(ids != own, jnp.exp2(score * exp2_scale - exp2_scale), 0.0)
        totals[...] += jnp.sum(expo, 0, keepdims=True)
        expo_all[zz, rows, :] = expo.astype(jnp.bfloat16)

    def pull_part(zz):
        ut_all[zz] = u_all[zz].T
        columns[:, :ROWS] = expo_all[zz]
        columns[:, ROWS:] = jnp.where(column_ids(zz) == partner[...], 1.0, 0.0).astype(jnp.bfloat16)
        both = dot(ut_all[zz], columns[...])
        pull_one[...] += both[:, :ROWS]
        pull_pos[...] += both[:, ROWS:]

    def send_on(way, hop, order):
        @pl.when(hop <= (3 if order < CHUNKS // 2 else 2))
        def _():
            ring_copy(way, hop, order).start()

        source = ring(-hop) if way == 0 else ring(hop)
        sib_copy(source, order_chunk(way, order)).start()

    def pass_on(hop, order):
        for way in range(2):
            source = ring(-hop) if way == 0 else ring(hop)
            ref = chunk_of(source, core, order_chunk(way, order))
            index = CHUNKS * (hop - 1) + order
            remote(ref, ref, ring_s.at[way, index], ring_r.at[way, index], sibling).wait_recv()
            send_on(way, hop, order)

    def events(k, part):
        hop = k // 2 + 1
        group = CHUNKS // 4
        for odd in range(2):
            orders = [odd * (CHUNKS // 2) + part * group + i for i in range(group)]

            @pl.when(lax.rem(k, 2) == odd)
            def _():
                for order in orders:
                    pass_on(hop, order)

    def gather_step(step, carry):
        group = jnp.minimum(step, 6)

        @pl.when(step != 6)
        def _():
            events(group, 0)

        @pl.when(step > 0)
        def _():
            pull_part(block_of(step - 1))

        @pl.when(step != 6)
        def _():
            events(group, 1)

        @pl.when((step == 3) & moves)
        def _():
            for copy in swap_raw():
                copy.start()

        @pl.when(step == 6)
        def _():
            @pl.when(moves)
            def _():
                for copy in swap_raw():
                    copy.wait_recv()

            summed_t[...] = (raw_clip[...].astype(jnp.float32) + raw_feat[...].astype(jnp.float32)).T

        zz = block_of(step)
        score_part(zz, core)
        for which in range(CHUNKS):
            sib_arrival(zz, which).wait_recv()
        score_part(zz, 1 - core)
        return carry

    lax.fori_loop(0, ZS, gather_step, 0)

    tot_all[z, core] = totals[...]
    others = [(dz, dc) for dz in (4, 3, 5, 2, 6, 1, 7, 0) for dc in range(2) if dz or dc]

    def total_copy(dz, dc):
        ref = tot_all.at[z, core]
        return remote(ref, ref, tot_s.at[dz, dc], tot_r.at[z, core], at(ring(dz), x, peer, lax.rem(core + dc, 2)))

    def total_arrival(zz, block):
        ref = tot_all.at[zz, block]
        return remote(ref, ref, tot_s.at[0, 0], tot_r.at[zz, block], sibling)

    loss_copy = remote(loss_stage, loss_ret, ret_s.at[PARTS], ret_r.at[PARTS], swapped)

    for dz, dc in others:
        total_copy(dz, dc).start()
    pull_part(block_of(ZS - 1))

    @pl.when(moves)
    def _():
        pl.semaphore_wait(barrier, PEERS)
        greet(at(z, 1 - x, peer, core), peers_in)


    inverse = 1.0 / totals[...]
    positive = jnp.sum(unit_t[...].astype(jnp.float32) * pull_pos[...], 0, keepdims=True)
    loss = logit_scale * (1.0 - positive) + jnp.log(totals[...])

    @pl.when(stays)
    def _():
        loss_out[...] = loss

    @pl.when(moves)
    def _():
        loss_stage[...] = loss
        loss_copy.start()
    acc[...] = inverse * pull_one[...] - 2.0 * pull_pos[...]
    factor_t = lax.rsqrt(jnp.sum(summed_t[...] * summed_t[...], 0, keepdims=True) + E * norm_eps)

    def second(zz, own):
        if not own:
            total_arrival(zz, core).wait_recv()
        total_arrival(zz, 1 - core).wait_recv()
        scale = 1.0 / jnp.concatenate([tot_all[zz, 0], tot_all[zz, 1]], 1)
        scaled = (ut_all[zz].astype(jnp.float32) * scale).astype(jnp.bfloat16)
        return dot(scaled, expo_all[zz])

    def second_hop(hop, carry):
        acc[...] += second(ring(-hop), False) + second(ring(hop), False)
        return carry

    acc[...] += second(z, True)
    for hop in range(1, 4):
        second_hop(hop, 0)
    last = ring(4)
    total_arrival(last, core).wait_recv()
    total_arrival(last, 1 - core).wait_recv()
    scale = 1.0 / jnp.concatenate([tot_all[last, 0], tot_all[last, 1]], 1)
    scaled = (ut_all[last].astype(jnp.float32) * scale).astype(jnp.bfloat16)
    scaled_last[...] = scaled

    def part_rows(part):
        return slice(part * PART, (part + 1) * PART)

    def ret_copy(part):
        rows = pl.ds(part * PART, PART)
        return remote(ret_stage.at[rows], ret.at[rows], ret_s.at[part], ret_r.at[part], swapped)

    def piece_rows(part, owner):
        return pl.ds(pl.multiple_of(part * PART + owner * PIECE, PIECE), PIECE)

    def rs_copy(part, d, crosses):
        owner = lax.rem(peer + d, PEERS)
        source = peer + PEERS if crosses else peer
        return remote(ret_stage.at[piece_rows(part, owner)], rs_buf.at[part, source], rs_s.at[part, d], rs_r.at[part, source],
                      at(z, 1 - x if crosses else x, owner, core))

    def rs_arrival(part, source):
        ref = rs_buf.at[part, source]
        return remote(ref, ref, rs_s.at[part, 0], rs_r.at[part, source], sibling)

    far_first = (4, 3, 5, 2, 6, 1, 7)

    @pl.when(stays)
    def _():
        pl.semaphore_wait(peers_in, 1)

    for part in range(PARTS):
        rows = part_rows(part)
        field = acc[:, rows]
        field += dot(scaled_last[...], expo_all[ring(4), :, rows])
        grad_unit = logit_scale * field
        summed_part = summed_t[:, rows]
        factor_part = factor_t[:, rows]
        along = jnp.sum(summed_part * grad_unit, 0, keepdims=True)
        grad = (factor_part * grad_unit - factor_part**3 * along * summed_part).T

        @pl.when(stays)
        def _():
            ret_stage[rows, :] = grad.astype(jnp.bfloat16)
            for d in far_first:
                rs_copy(part, d, False).start()
            seg_out[0, rows, :] = grad
            rs_buf[part, peer] = ret_stage[piece_rows(part, peer), :]

        @pl.when(moves)
        def _():
            ret_stage[rows, :] = grad.astype(jnp.bfloat16)
            for d in far_first + (0,):
                rs_copy(part, d, True).start()

    @pl.when(moves)
    def _():
        for part in range(PARTS):
            ret_copy(part).start()

    for way in range(2):
        for index in range(RING_COPIES):
            ring_copy(way, index // CHUNKS, index % CHUNKS).wait_send()
    for zz in range(ZS):
        for which in range(CHUNKS):
            sib_copy(zz, which).wait_send()
    for dz, dc in others:
        total_copy(dz, dc).wait_send()

    @pl.when(moves)
    def _():
        for which in range(CHUNKS):
            swap_unit(which, x).wait_send()
        swap_pair.wait_send()
        for copy in swap_raw():
            copy.wait_send()
        loss_copy.wait_send()

    def gathered_rows(part, owner):
        return gathered.at[pl.ds(pl.multiple_of(part * PART + owner * PIECE, PIECE), PIECE)]

    def ag_copy(part, d):
        ref = gathered_rows(part, peer)
        return remote(ref, ref, ag_s.at[part, d], ag_r.at[part, peer], at(z, x, lax.rem(peer + d, PEERS), core))

    def ag_arrival(part, source):
        ref = gathered_rows(part, source)
        return remote(ref, ref, ag_s.at[part, 0], ag_r.at[part, source], sibling)

    def last_copy(d):
        ref = gathered_rows(PARTS - 1, peer)
        return remote(ref, ref, last_s.at[d], last_r.at[peer], at(z, x, lax.rem(peer + d, PEERS), 1 - core))

    def last_arrival(source):
        ref = gathered_rows(PARTS - 1, source)
        return remote(ref, ref, last_s.at[0], last_r.at[source], sibling)

    def fin_copy(part):
        ref = gathered.at[pl.ds(part * PART, PART)]
        return remote(ref, ref, fin_s.at[part], fin_r.at[part], sibling)

    @pl.when(stays)
    def _():
        for part in range(PARTS):
            for d in far_first[::-1]:
                rs_arrival(part, lax.rem(peer + d, PEERS)).wait_recv()
            for d in range(PEERS):
                rs_arrival(part, PEERS + lax.rem(peer + d, PEERS)).wait_recv()
            reduced = rs_buf[part, 0].astype(jnp.float32)
            for source in range(1, 2 * PEERS):
                reduced += rs_buf[part, source].astype(jnp.float32)
            gathered[piece_rows(part, peer), :] = reduced.astype(jnp.bfloat16)
            for d in far_first:
                ag_copy(part, d).start()
                if part == PARTS - 1:
                    last_copy(d).start()
            if part == PARTS - 1:
                last_copy(0).start()
        for part in range(PARTS):
            for d in far_first:
                rs_copy(part, d, False).wait_send()
        for part in range(PARTS):
            for d in far_first[::-1]:
                ag_arrival(part, lax.rem(peer + PEERS - d, PEERS)).wait_recv()
            if part < PARTS - 1:
                fin_copy(part).start()
        for part in range(PARTS):
            for d in far_first:
                ag_copy(part, d).wait_send()
            if part < PARTS - 1:
                fin_copy(part).wait_send()
        for d in range(PEERS):
            last_copy(d).wait_send()

    @pl.when(moves)
    def _():
        loss_copy.wait_recv()
        loss_out[...] = loss_ret[...]
        for part in range(PARTS):
            rows = part_rows(part)
            ret_copy(part).wait_recv()
            seg_out[0, rows, :] = ret[rows, :].astype(jnp.float32)
        for part in range(PARTS):
            ret_copy(part).wait_send()
            for d in range(PEERS):
                rs_copy(part, d, True).wait_send()
        for part in range(PARTS):
            if part < PARTS - 1:
                fin_copy(part).wait_recv()
        for d in (0,) + far_first[::-1]:
            last_arrival(lax.rem(peer + PEERS - d, PEERS)).wait_recv()


def hand_over(loss_in, seg_in, sum_in, loss_out, seg_out, clip_out, wide, sems):
    copies = [
        pltpu.make_async_copy(seg_in, seg_out, sems.at[0]),
        pltpu.make_async_copy(loss_in, loss_out, sems.at[1]),
    ]
    for copy in copies:
        copy.start()
    for part in range(PARTS):
        rows = pl.ds(part * PART, PART)
        wide[rows, :] = sum_in[rows, :].astype(jnp.float32)
        copies.append(pltpu.make_async_copy(wide.at[rows], clip_out.at[rows], sems.at[2 + part]))
        copies[-1].start()
    for copy in copies:
        copy.wait()


def on_device(clip_embed, seg_feats, pair_index):
    bf16, f32, i32 = jnp.bfloat16, jnp.float32, jnp.int32
    vmem = pl.BlockSpec(memory_space=pltpu.VMEM)
    anywhere = pl.BlockSpec(memory_space=pl.ANY)
    hbm = pl.BlockSpec(memory_space=pltpu.HBM)
    dma = pltpu.SemaphoreType.DMA
    loss, seg, total = pl.pallas_call(
        kernel,
        name="ntxent",
        out_shape=(
            pltpu.VMEM((1, ROWS), f32),
            pltpu.VMEM((1, ROWS, E), f32),
            pltpu.VMEM((ROWS, E), bf16),
        ),
        in_specs=[hbm] * 3,
        out_specs=(vmem,) * 3,
        scratch_shapes=[
            pltpu.VMEM((ZS, PAIR, E), bf16),
            pltpu.VMEM((ZS, E, PAIR), bf16),
            pltpu.VMEM((ZS, PAIR, ROWS), bf16),
            pltpu.VMEM((PAIR, 2 * ROWS), bf16),
            pltpu.VMEM((E, PAIR), bf16),
            pltpu.VMEM((ZS, 2, 1, ROWS), f32),
            pltpu.VMEM((E, ROWS), bf16),
            pltpu.VMEM((ROWS, E), bf16),
            pltpu.VMEM((ROWS, E), bf16),
            pltpu.VMEM((ROWS, E), bf16),
            pltpu.VMEM((ROWS, E), bf16),
            pltpu.VMEM((ROWS, E), bf16),
            pltpu.VMEM((1, ROWS), i32),
            pltpu.VMEM((1, ROWS), f32),
            pltpu.VMEM((E, ROWS), f32),
            pltpu.VMEM((E, ROWS), f32),
            pltpu.VMEM((E, ROWS), f32),
            pltpu.VMEM((E, ROWS), f32),
            pltpu.VMEM((ROWS, E), bf16),
            pltpu.VMEM((ROWS, E), bf16),
            pltpu.VMEM((1, ROWS), f32),
            pltpu.VMEM((1, ROWS), f32),
            pltpu.VMEM((PARTS, 2 * PEERS, PIECE, E), bf16),
            dma((3, CHUNKS)),
            dma((CHUNKS + 3,)), dma((CHUNKS + 3,)),
            dma((2, RING_COPIES)), dma((2, RING_COPIES)),
            dma((ZS, CHUNKS)), dma((ZS, CHUNKS)),
            dma((ZS, 2)), dma((ZS, 2)),
            dma((PARTS + 1,)), dma((PARTS + 1,)),
            dma((PARTS, PEERS)), dma((PARTS, 2 * PEERS)),
            dma((PARTS, PEERS)), dma((PARTS, PEERS)),
            dma((PEERS,)), dma((PEERS,)),
            dma((PARTS,)), dma((PARTS,)),
            pltpu.SemaphoreType.REGULAR, pltpu.SemaphoreType.REGULAR, pltpu.SemaphoreType.REGULAR,
        ],
        compiler_params=pltpu.CompilerParams(
            collective_id=0, has_side_effects=True, vmem_limit_bytes=56 * 2**20
        ),
    )(clip_embed, seg_feats, pair_index)
    return pl.pallas_call(
        hand_over,
        name="hand_over",
        out_shape=(
            jax.ShapeDtypeStruct((1, ROWS), f32),
            jax.ShapeDtypeStruct((1, ROWS, E), f32),
            jax.ShapeDtypeStruct((ROWS, E), f32),
        ),
        in_specs=[vmem] * 3,
        out_specs=(anywhere,) * 3,
        scratch_shapes=[pltpu.VMEM((ROWS, E), f32), dma((2 + PARTS,))],
        compiler_params=pltpu.CompilerParams(vmem_limit_bytes=4 * 2**20),
    )(loss, seg, total)


def solution(mesh):
    placed = (P("clip", None), P("tm", "clip", None), P("tm", "clip"))
    return jax.shard_map(
        on_device,
        mesh=mesh,
        in_specs=placed,
        out_specs=(P("tm", "clip"), P("tm", "clip", None), P("clip", None)),
        check_vma=False,
    )
```
